32 devices in a mesh: obs: 8 (over z, x), par: 4 (over y, core).
Axes of the slice: x: 2, y: 2, z: 4, core: 2. Of those that a mesh axis runs over, the one named last changes fastest.
Arguments:
- operator: bfloat16 [4096, 65536], P('obs', 'par'), as said below
- targets: float32 [16, 4096], P(None, 'obs'), may hold values from -6 to 6
- start: float32 [16, 65536], P(None, 'par'), may hold values from -3 to 3
Outputs:
- solution: float32 [16, 65536], P(None, 'par')
- residual: float32 [16, 4096], P(None, 'obs')
The draws below stay inside these ranges and needn't reach their ends.
Inputs may be any that keep to these rules, and one draw needn't show every extreme that they name: `operator`: entries are the product of an independent draw, a scale of each row and a scale of each column, divided by the square root of 65536.
All inputs are finite; a program needn't handle non-finite values.
Results may differ from the reference program's by a relative error of at most 0.00775.
Values may be sent and summed in bfloat16 or wider, within the bound.
No kernel may reach another device: no remote copies, remote signals or barrier semaphores. Data moves between devices by JAX's collectives and lax.ppermute only.
A program may use at most 64 MiB of HBM per device.

```python
import jax
import jax.numpy as jnp
from jax import lax

PARAMS = 65536
SCEN = 16
ITERS = 4
ROWS = 4096


def draw_operator(key, part):
    key = jax.random.fold_in(key, 11)
    key_base, key_rows, key_cols = jax.random.split(key, 3)
    base = jax.random.normal(key_base, (ROWS, PARAMS), jnp.float32)
    row_scale = jnp.exp(jax.random.uniform(key_rows, (ROWS, 1), jnp.float32, 0.0, 2.3025851))
    col_scale = jnp.exp(jax.random.uniform(key_cols, (1, PARAMS), jnp.float32, -0.6931472, 0.6931472))
    return (base * row_scale * col_scale / jnp.sqrt(jnp.float32(PARAMS))).astype(jnp.bfloat16)


def block_scale(own_key, shape, pieces, low, top_value):
    gain = 1.0
    for axis_at, parts in pieces:
        draws = jax.random.uniform(jax.random.fold_in(jax.random.fold_in(own_key, 6), axis_at), (parts,), jnp.float32, low / len(pieces), top_value / len(pieces))
        gain = gain * jnp.repeat(jnp.exp(draws), shape[axis_at] // parts).reshape((-1,) + (1,) * (len(shape) - 1 - axis_at))
    return gain


def scatter_about(own_key, extent, deviation, limit, cuts=(), held_as=jnp.bfloat16):
    level = block_scale(own_key, extent, cuts, -0.22, 0.18) if cuts else 1.0
    entries = jax.random.normal(own_key, extent, jnp.float32) * deviation * level
    return jnp.minimum(jnp.maximum(entries, -limit), limit).astype(held_as)


def setup_inputs(seed: int = 0) -> dict:
    streams_of = jax.random.split(jax.random.key(seed), 4)
    return {
        "operator": draw_operator(jax.random.fold_in(streams_of[3], 71), 0),
        "targets": scatter_about(streams_of[1], (SCEN, ROWS), 1.0, 6.0, ((1, 8),), jnp.float32),
        "start": scatter_about(streams_of[2], (SCEN, PARAMS), 0.2, 3.0, ((1, 4),), jnp.float32),
    }


def forward(operator, vector):
    return lax.dot_general(vector.astype(jnp.bfloat16), operator, (((1,), (1,)), ((), ())), preferred_element_type=jnp.float32)


def backward(operator, vector):
    return jnp.dot(vector.astype(jnp.bfloat16), operator, preferred_element_type=jnp.float32)


def reference(operator, targets, start):
    residual = targets - forward(operator, start)
    gradient = backward(operator, residual)
    direction = gradient
    gamma = jnp.sum(gradient * gradient, axis=1, keepdims=True)

    def step(index, carry):
        solution, residual, direction, gamma = carry
        image = forward(operator, direction)
        delta = jnp.sum(image * image, axis=1, keepdims=True)
        alpha = gamma / delta
        solution = solution + alpha * direction
        residual = residual - alpha * image
        gradient = backward(operator, residual)
        gamma_new = jnp.sum(gradient * gradient, axis=1, keepdims=True)
        direction = gradient + (gamma_new / gamma) * direction
        return (solution, residual, direction, gamma_new)

    solution, residual, direction, gamma = lax.fori_loop(0, ITERS, step, (start, residual, direction, gamma))
    return solution, residual
```

```python
import functools

import jax
import jax.numpy as jnp
from jax import lax
from jax.experimental import pallas as pl
from jax.experimental.pallas import tpu as pltpu
from jax.sharding import PartitionSpec as P

ITERS = 4
LANES = 128
F32 = jnp.float32
BF16 = jnp.bfloat16
VMEM = pl.BlockSpec(memory_space=pltpu.VMEM)
SMEM = pl.BlockSpec(memory_space=pltpu.SMEM)
HBM = pl.BlockSpec(memory_space=pl.ANY)


def params(mebibytes=32):
    return pltpu.CompilerParams(vmem_limit_bytes=mebibytes << 20)


def cost(scen, rows, columns):
    return pl.CostEstimate(
        flops=2 * 16 * scen * rows * columns, bytes_accessed=2 * rows * columns, transcendentals=0
    )


def load_kernel(chunk, op_hbm, start_hbm, op_ref, image_ref, start_ref, sems):
    pieces = op_ref.shape[1] // chunk
    copies = [pltpu.make_async_copy(start_hbm, start_ref, sems.at[pieces])]
    for k in range(pieces):
        at = pl.ds(k * chunk, chunk)
        copies.append(pltpu.make_async_copy(op_hbm.at[:, at], op_ref.at[:, at], sems.at[k]))
    for copy in copies:
        copy.start()
    copies[0].wait()
    total = jnp.zeros(image_ref.shape, F32)
    for k in range(pieces):
        copies[k + 1].wait()
        at = pl.ds(k * chunk, chunk)
        total += lax.dot_general(
            start_ref[:, at].astype(BF16), op_ref[:, at], (((1,), (1,)), ((), ())), preferred_element_type=F32
        )
    image_ref[...] = total


def load(operator, start):
    rows, columns = operator.shape
    scen = start.shape[0]
    chunk = min(2048, columns)
    return pl.pallas_call(
        functools.partial(load_kernel, chunk),
        out_shape=(
            jax.ShapeDtypeStruct(operator.shape, BF16),
            jax.ShapeDtypeStruct((scen, rows), F32),
        ),
        in_specs=[HBM, HBM],
        out_specs=(VMEM, VMEM),
        scratch_shapes=[pltpu.VMEM(start.shape, F32), pltpu.SemaphoreType.DMA((columns // chunk + 1,))],
        compiler_params=params(),
        cost_estimate=cost(scen, rows, columns),
    )(operator, start)


def backward_kernel(chunk, at_ref, op_ref, w_ref, norm_ref, out_ref):
    width = out_ref.shape[1] - (LANES if norm_ref is not None else 0)
    scen = out_ref.shape[0]
    w = w_ref[...]
    base = at_ref[0] * width
    for k in range(width // chunk):
        at = pl.ds(pl.multiple_of(base + k * chunk, chunk), chunk)
        both = jnp.dot(w, op_ref[:, at], preferred_element_type=F32)
        out_ref[:, k * chunk : (k + 1) * chunk] = (both[:scen] + both[scen:]).astype(out_ref.dtype)
    if norm_ref is not None:
        out_ref[:, width:] = norm_ref[...]


def backward(at, op, w, norm, width):
    scen = w.shape[0] // 2
    chunk = min(1024, width)
    if norm is None:
        body = lambda at_ref, op_ref, w_ref, out_ref: backward_kernel(chunk, at_ref, op_ref, w_ref, None, out_ref)
        out = jax.ShapeDtypeStruct((scen, width), F32)
        more = ()
    else:
        body = functools.partial(backward_kernel, chunk)
        out = jax.ShapeDtypeStruct((scen, width + LANES), BF16)
        more = (norm,)
    return pl.pallas_call(
        body,
        out_shape=out,
        in_specs=[SMEM, VMEM, VMEM] + [VMEM] * len(more),
        out_specs=VMEM,
        compiler_params=params(),
        cost_estimate=cost(scen, op.shape[0], width),
    )(at.reshape(1), op, w, *more)


def forward_kernel(at_ref, op_ref, v_ref, sum_ref, out_ref):
    width = v_ref.shape[1]
    rows = op_ref.shape[0]
    v = v_ref[...]
    at = pl.ds(pl.multiple_of(at_ref[0] * width, width), width)
    image = lax.dot_general(v, op_ref[:, at], (((1,), (1,)), ((), ())), preferred_element_type=F32)
    wide = v.astype(F32)
    square = wide * wide
    norm = square[:, :LANES]
    for k in range(1, width // LANES):
        norm += square[:, k * LANES : (k + 1) * LANES]
    if sum_ref is not None:
        image += sum_ref[:, :rows]
        norm += sum_ref[:, rows:]
    out_ref[:, :rows] = image
    out_ref[:, rows:] = norm


def forward(at, op, v, total):
    scen, width = v.shape
    rows = op.shape[0]
    if total is None:
        body = lambda at_ref, op_ref, v_ref, out_ref: forward_kernel(at_ref, op_ref, v_ref, None, out_ref)
        more = ()
    else:
        body = forward_kernel
        more = (total,)
    return pl.pallas_call(
        body,
        out_shape=jax.ShapeDtypeStruct((scen, rows + LANES), F32),
        in_specs=[SMEM, VMEM, VMEM] + [VMEM] * len(more),
        out_specs=VMEM,
        compiler_params=params(),
        cost_estimate=cost(scen, rows, width),
    )(at.reshape(1), op, v, *more)


def exchange(value, axis, size, distance):
    return lax.ppermute(value, axis, [(i, i ^ distance) for i in range(size)])


def stages(size, stride=1):
    while stride < size:
        members = 4 if size // stride % 4 == 0 else 2
        yield stride, members
        stride *= members


def tree(parts):
    if len(parts) == 2:
        return parts[0] + parts[1]
    return (parts[0] + parts[1]) + (parts[2] + parts[3])


def sum_over(value, axis, size, stride=1):
    for stride, members in stages(size, stride):
        value = tree([value] + [exchange(value, axis, size, k * stride) for k in range(1, members)])
    return value


def rounded(value):
    return lax.reduce_precision(value, exponent_bits=8, mantissa_bits=7)


def split3(value):
    high = rounded(value)
    rest = value - high
    middle = rounded(rest)
    return high.astype(BF16), middle.astype(BF16), rounded(rest - middle).astype(BF16)


def norm_block(value):
    terms = split3(value)
    lane = lax.broadcasted_iota(jnp.int32, (value.shape[0], LANES), 1)
    block = jnp.zeros((value.shape[0], LANES), BF16)
    for k, term in enumerate(terms):
        block = jnp.where(lane == k, term, block)
    return block


def norm_of(block):
    wide = block.astype(F32)
    return (wide[:, 0:1] + wide[:, 1:2]) + wide[:, 2:3]


def shards(n_obs, n_par, operator, targets, start):
    rows, columns = operator.shape
    near = 4 if n_obs % 4 == 0 else n_obs
    width = columns // near
    me = lax.axis_index("obs")
    own = me % near

    def gradient_sum(w, norm):
        sent = {d: backward(own ^ d, op, w, norm_block(norm), width) for d in reversed(range(1, near))}
        got = {d: exchange(sent[d], "obs", n_obs, d) for d in sent}
        mine = backward(own, op, w, None, width)
        total = tree([mine] + [got[d][:, :width].astype(F32) for d in range(1, near)])
        norms = tree([norm] + [norm_of(got[d][:, width:]) for d in range(1, near)])
        for stride, members in stages(n_obs, near):
            total = rounded(total)
            both = jnp.concatenate([total.astype(BF16), norm_block(norms)], axis=1)
            got = [exchange(both, "obs", n_obs, k * stride) for k in range(1, members)]
            total = tree([total] + [part[:, :width].astype(F32) for part in got])
            norms = tree([norms] + [norm_of(part[:, width:]) for part in got])
        return total, norms

    def image_of(mine):
        got = {d: exchange(mine, "obs", n_obs, d) for d in reversed(range(1, near))}
        total = forward(own, op, mine, None)
        for d in got:
            total = forward(own ^ d, op, got[d], total)
        total = sum_over(total, "par", n_par)
        got[0] = mine
        return total[:, :rows], got, jnp.sum(total[:, rows:], axis=1, keepdims=True)

    def whole(pieces):
        ordered = [None] * near
        stacked = jnp.stack([pieces[d] for d in range(near)])
        for k in range(near):
            ordered[k] = lax.dynamic_index_in_dim(stacked, own ^ k, 0, keepdims=False)
        return jnp.concatenate(ordered, axis=1)

    def high_low(value):
        high = rounded(value)
        return jnp.concatenate([high, rounded(value - high)], axis=0).astype(BF16)

    op, first = load(operator, start)
    residual = targets - sum_over(first, "par", n_par)
    gradient, _ = gradient_sum(high_low(residual), jnp.zeros((start.shape[0], 1), F32))
    solution = start
    for index in range(ITERS):
        product, pieces, gamma_new = image_of(rounded(gradient).astype(BF16))
        if index == 0:
            image = product
            direction = whole(pieces).astype(F32)
        else:
            beta = gamma_new / gamma
            image = product + beta * image
            direction = whole(pieces).astype(F32) + beta * direction
        gamma = gamma_new
        delta = jnp.sum(image * image, axis=1, keepdims=True)
        if index < ITERS - 1:
            change, delta = gradient_sum(high_low(image), delta)
        else:
            delta = sum_over(jnp.broadcast_to(delta, (delta.shape[0], LANES)), "obs", n_obs)[:, :1]
        alpha = gamma / delta
        if index < ITERS - 1:
            gradient = gradient - alpha * change
        solution = solution + alpha * direction
        residual = residual - alpha * image
    return (solution, residual)


def solution(mesh):
    return jax.shard_map(
        functools.partial(shards, mesh.shape["obs"], mesh.shape["par"]),
        mesh=mesh,
        in_specs=(P("obs", "par"), P(None, "obs"), P(None, "par")),
        out_specs=(P(None, "par"), P(None, "obs")),
        check_vma=False,
    )
```

```python
import functools

import jax
import jax.numpy as jnp
from jax import lax
from jax.experimental import pallas as pl
from jax.experimental.pallas import tpu as pltpu
from jax.sharding import PartitionSpec as P

ITERS = 4
LANES = 128
F32 = jnp.float32
BF16 = jnp.bfloat16
VMEM = pl.BlockSpec(memory_space=pltpu.VMEM)
ANY = pl.BlockSpec(memory_space=pl.ANY)


def shape(*sizes, dtype=F32):
    return jax.ShapeDtypeStruct(sizes, dtype)


def call(body, out, args, specs=None, scratch=(), flops=0, bytes_accessed=1 << 18):
    return pl.pallas_call(
        body,
        out_shape=out,
        in_specs=specs if specs is not None else [VMEM] * len(args),
        out_specs=jax.tree.map(lambda _: VMEM, out),
        scratch_shapes=scratch,
        compiler_params=pltpu.CompilerParams(vmem_limit_bytes=24 << 20),
        cost_estimate=pl.CostEstimate(flops=flops, bytes_accessed=bytes_accessed, transcendentals=0),
    )(*args)


def operator_cost(rows, columns):
    return {"flops": 512 * rows * columns, "bytes_accessed": 2 * rows * columns}


def tree(parts):
    if len(parts) == 1:
        return parts[0]
    if len(parts) == 2:
        return parts[0] + parts[1]
    return (parts[0] + parts[1]) + (parts[2] + parts[3])


def lane_total(value):
    return jnp.broadcast_to(jnp.sum(value, axis=1, keepdims=True), (value.shape[0], LANES))


def pack_norm(value):
    high = value.astype(BF16).astype(F32)
    rest = value - high
    middle = rest.astype(BF16).astype(F32)
    lane = lax.broadcasted_iota(jnp.int32, value.shape, 1)
    zero = jnp.zeros_like(value)
    return jnp.where(
        lane == 0, high, jnp.where(lane == 1, middle, jnp.where(lane == 2, rest - middle, zero))
    ).astype(BF16)


def unpack_norm(block):
    return lane_total(block.astype(F32))


def split(value, out_ref):
    scen = value.shape[0]
    high = value.astype(BF16)
    out_ref[:scen, :] = high
    out_ref[scen:, :] = (value - high.astype(F32)).astype(BF16)


def load_kernel(chunk, op_hbm, start_hbm, op_ref, image_ref, start_ref, sems):
    pieces = op_ref.shape[1] // chunk
    copies = [pltpu.make_async_copy(start_hbm, start_ref, sems.at[pieces])]
    for k in range(pieces):
        at = pl.ds(k * chunk, chunk)
        copies.append(pltpu.make_async_copy(op_hbm.at[:, at], op_ref.at[:, at], sems.at[k]))
    for copy in copies:
        copy.start()
    copies[0].wait()
    total = jnp.zeros(image_ref.shape, F32)
    for k in range(pieces):
        copies[k + 1].wait()
        at = pl.ds(k * chunk, chunk)
        total += lax.dot_general(
            start_ref[:, at].astype(BF16), op_ref[:, at], (((1,), (1,)), ((), ())), preferred_element_type=F32
        )
    image_ref[...] = total


def load(operator, start):
    rows, columns = operator.shape
    chunk = min(2048, columns)
    return call(
        functools.partial(load_kernel, chunk),
        (shape(rows, columns, dtype=BF16), shape(start.shape[0], rows)),
        (operator, start),
        [ANY, ANY],
        [pltpu.VMEM(start.shape, F32), pltpu.SemaphoreType.DMA((columns // chunk + 1,))],
        **operator_cost(rows, columns),
    )


def place(near, distance):
    return (lax.axis_index("obs") & (near - 1)) ^ distance


def backward_kernel(near, distance, chunk, op_ref, w_ref, *refs):
    out_ref = refs[-1]
    scen = out_ref.shape[0]
    width = out_ref.shape[1] - LANES * (len(refs) - 1)
    w = w_ref[...]
    base = place(near, distance) * width
    for k in range(width // chunk):
        at = pl.ds(pl.multiple_of(base + k * chunk, chunk), chunk)
        both = jnp.dot(w, op_ref[:, at], preferred_element_type=F32)
        out_ref[:, k * chunk : (k + 1) * chunk] = (both[:scen] + both[scen:]).astype(out_ref.dtype)
    for norm_ref in refs[:-1]:
        out_ref[:, width:] = norm_ref[...]


def backward(near, distance, op, w, *norm):
    width = op.shape[1] // near
    scen = w.shape[0] // 2
    out = shape(scen, width + LANES, dtype=BF16) if norm else shape(scen, width)
    return call(
        functools.partial(backward_kernel, near, distance, min(1024, width)),
        out,
        (op, w, *norm),
        **operator_cost(op.shape[0], width),
    )


def forward_kernel(near, distance, op_ref, v_ref, *refs):
    out_ref = refs[-1]
    width = v_ref.shape[1]
    rows = op_ref.shape[0]
    v = v_ref[...]
    at = pl.ds(pl.multiple_of(place(near, distance) * width, width), width)
    image = lax.dot_general(v, op_ref[:, at], (((1,), (1,)), ((), ())), preferred_element_type=F32)
    wide = v.astype(F32)
    square = wide * wide
    norm = square[:, :LANES]
    for k in range(1, width // LANES):
        norm += square[:, k * LANES : (k + 1) * LANES]
    for sum_ref in refs[:-1]:
        image += sum_ref[:, :rows]
        norm += sum_ref[:, rows:]
    out_ref[:, :rows] = image
    out_ref[:, rows:] = norm


def forward(near, distance, op, v, *total):
    scen, width = v.shape
    rows = op.shape[0]
    return call(
        functools.partial(forward_kernel, near, distance),
        shape(scen, rows + LANES),
        (op, v, *total),
        **operator_cost(rows, width),
    )


def first_kernel(targets_ref, *refs):
    *part_refs, residual_ref, w_ref, norm_ref, packed_ref = refs
    residual = targets_ref[...] - tree([ref[...] for ref in part_refs])
    residual_ref[...] = residual
    norm_ref[...] = jnp.zeros(norm_ref.shape, F32)
    packed_ref[...] = jnp.zeros(packed_ref.shape, BF16)
    split(residual, w_ref)


def image_kernel(later, last, *refs):
    outs = 4 + (not last) * 2
    ins, (image_ref, gamma_ref, beta_ref, norm_ref, *more_refs) = refs[:-outs], refs[-outs:]
    if later:
        old_ref, old_gamma_ref, *ins = ins
    total = tree([ref[...] for ref in ins])
    rows = image_ref.shape[1]
    image = total[:, :rows]
    gamma = lane_total(total[:, rows:])
    beta = jnp.zeros_like(gamma)
    if later:
        beta = gamma / old_gamma_ref[...]
        image += jnp.concatenate([beta] * (rows // LANES), axis=1) * old_ref[...]
    image_ref[...] = image
    gamma_ref[...] = gamma
    beta_ref[...] = beta
    norm = lane_total(image * image)
    norm_ref[...] = norm
    if not last:
        packed_ref, w_ref = more_refs
        packed_ref[...] = pack_norm(norm)
        split(image, w_ref)


def near_kernel(mine_ref, norm_ref, *refs):
    *got_refs, out_ref = refs
    width = mine_ref.shape[1]
    total = tree([mine_ref[...]] + [ref[:, :width].astype(F32) for ref in got_refs])
    norm = tree([norm_ref[...]] + [unpack_norm(ref[:, width:]) for ref in got_refs])
    out_ref[:, :width] = total.astype(BF16)
    out_ref[:, width:] = pack_norm(norm)


def far_kernel(*refs):
    *got_refs, out_ref = refs
    width = out_ref.shape[1] - LANES
    out_ref[:, :width] = tree([ref[:, :width].astype(F32) for ref in got_refs]).astype(BF16)
    out_ref[:, width:] = pack_norm(tree([unpack_norm(ref[:, width:]) for ref in got_refs]))


def gradient_kernel(later, *refs):
    *ins, gradient_ref, rounded_ref, alpha_ref = refs
    if later:
        old_ref, gamma_ref, *ins = ins
    width = gradient_ref.shape[1]
    total = tree([ref[:, :width].astype(F32) for ref in ins])
    if later:
        alpha = gamma_ref[...] / tree([unpack_norm(ref[:, width:]) for ref in ins])
        alpha_ref[...] = alpha
        total = old_ref[...] - jnp.concatenate([alpha] * (width // LANES), axis=1) * total
    else:
        alpha_ref[...] = jnp.zeros(alpha_ref.shape, F32)
    gradient_ref[...] = total
    rounded_ref[...] = total.astype(BF16)


def directions_kernel(near, width, start_ref, *refs):
    *ins, direction_ref, solution_ref = refs
    alphas = ins[: ITERS - 1]
    betas = ins[ITERS - 1 : 2 * ITERS - 1]
    pieces = ins[2 * ITERS - 1 :]
    for d in range(near):
        base = place(near, d) * width
        for k in range(width // LANES):
            at = pl.ds(pl.multiple_of(base + k * LANES, LANES), LANES)
            here = slice(k * LANES, (k + 1) * LANES)
            solution = start_ref[:, at]
            direction = pieces[d][:, here].astype(F32)
            for index in range(1, ITERS):
                solution += alphas[index - 1][...] * direction
                direction = pieces[index * near + d][:, here].astype(F32) + betas[index][...] * direction
            direction_ref[:, at] = direction
            solution_ref[:, at] = solution


def last_kernel(parts, gamma_ref, direction_ref, base_ref, residual_ref, *refs):
    *ins, out_ref, out_residual_ref = refs
    norms = ins[:parts]
    alphas = ins[parts : parts + ITERS - 1]
    images = ins[parts + ITERS - 1 :]
    alpha = gamma_ref[...] / tree([ref[...] for ref in norms])

    def step(k, _):
        at = pl.ds(pl.multiple_of(k * LANES, LANES), LANES)
        out_ref[:, at] = base_ref[:, at] + alpha * direction_ref[:, at]
        return 0

    lax.fori_loop(0, out_ref.shape[1] // LANES, step, 0, unroll=8)
    residual = residual_ref[...]
    rows = residual.shape[1]
    for index in range(ITERS):
        factor = alpha if index == ITERS - 1 else alphas[index][...]
        residual -= jnp.concatenate([factor] * (rows // LANES), axis=1) * images[index][...]
    out_residual_ref[...] = residual


def exchange(value, axis, size, distance):
    return lax.ppermute(value, axis, [(i, i ^ distance) for i in range(size)])


def stages(size, stride=1):
    found = []
    while stride < size:
        members = 4 if size // stride % 4 == 0 else 2
        found.append((stride, members))
        stride *= members
    return found


def exchanged(value, axis, size, stride, members):
    return [value] + [exchange(value, axis, size, k * stride) for k in range(1, members)]


def parts_over(value, axis, size):
    parts = [value]
    for stride, members in stages(size):
        parts = exchanged(tree(parts), axis, size, stride, members)
    return parts


def shards(n_obs, n_par, operator, targets, start):
    rows, columns = operator.shape
    scen = start.shape[0]
    near = 4 if n_obs % 4 == 0 else n_obs
    width = columns // near
    lanes = shape(scen, LANES)
    image_shape = shape(scen, rows)
    term_shape = shape(2 * scen, rows, dtype=BF16)

    def gradient_parts(w, norm, packed):
        sent = {d: backward(near, d, op, w, packed) for d in reversed(range(1, near))}
        got = {d: exchange(sent[d], "obs", n_obs, d) for d in sent}
        mine = backward(near, 0, op, w)
        both = shape(scen, width + LANES, dtype=BF16)
        value = call(near_kernel, both, (mine, norm, *(got[d] for d in range(1, near))))
        parts = [value]
        for index, (stride, members) in enumerate(stages(n_obs, near)):
            if index:
                value = call(far_kernel, both, parts)
            parts = exchanged(value, "obs", n_obs, stride, members)
        return parts

    def image_parts(mine):
        got = {d: exchange(mine, "obs", n_obs, d) for d in reversed(range(1, near))}
        total = forward(near, 0, op, mine)
        for d in got:
            total = forward(near, d, op, got[d], total)
        return parts_over(total, "par", n_par), [mine] + [got[d] for d in range(1, near)]

    op, first = load(operator, start)
    packed_lanes = shape(scen, LANES, dtype=BF16)
    residual, w, norm, packed = call(
        first_kernel, (image_shape, term_shape, lanes, packed_lanes), (targets, *parts_over(first, "par", n_par))
    )
    images, alphas, betas, pieces = [], [], [], []
    gradient = gamma = None
    for index in range(ITERS):
        parts = gradient_parts(w, norm, packed)
        gradient, rounded, alpha = call(
            functools.partial(gradient_kernel, index > 0),
            (shape(scen, width), shape(scen, width, dtype=BF16), lanes),
            ((gradient, gamma) if index else ()) + tuple(parts),
        )
        alphas += [alpha] if index else []
        parts, got = image_parts(rounded)
        pieces += got
        last = index == ITERS - 1
        image, gamma, beta, norm, *more = call(
            functools.partial(image_kernel, index > 0, last),
            (image_shape, lanes, lanes, lanes) + (() if last else (packed_lanes, term_shape)),
            ((image, gamma) if index else ()) + tuple(parts),
        )
        if not last:
            packed, w = more
        images.append(image)
        betas.append(beta)

    norms = parts_over(norm, "obs", n_obs)
    direction, base = call(
        functools.partial(directions_kernel, near, width),
        (shape(scen, columns), shape(scen, columns)),
        (start, *alphas, *betas, *pieces),
        flops=1 << 22,
        bytes_accessed=6 << 20,
    )
    return call(
        functools.partial(last_kernel, len(norms)),
        (shape(scen, columns), image_shape),
        (gamma, direction, base, residual, *norms, *alphas, *images),
    )


def solution(mesh):
    return jax.shard_map(
        functools.partial(shards, mesh.shape["obs"], mesh.shape["par"]),
        mesh=mesh,
        in_specs=(P("obs", "par"), P(None, "obs"), P(None, "par")),
        out_specs=(P(None, "par"), P(None, "obs")),
        check_vma=False,
    )
```

```python
import functools

import jax
import jax.numpy as jnp
from jax import lax
from jax.experimental import pallas as pl
from jax.experimental.pallas import tpu as pltpu
from jax.sharding import PartitionSpec as P

ITERS = 4
ADD_FLOPS = 1 << 28
LANES = 128
F32 = jnp.float32
BF16 = jnp.bfloat16
VMEM = pl.BlockSpec(memory_space=pltpu.VMEM)
ANY = pl.BlockSpec(memory_space=pl.ANY)


def shape(*sizes, dtype=F32):
    return jax.ShapeDtypeStruct(sizes, dtype)


def call(body, out, args, specs=None, scratch=(), flops=0, limit=24 << 20):
    return pl.pallas_call(
        body,
        out_shape=out,
        in_specs=specs if specs is not None else [VMEM] * len(args),
        out_specs=jax.tree.map(lambda _: VMEM, out),
        scratch_shapes=scratch,
        compiler_params=pltpu.CompilerParams(vmem_limit_bytes=limit),
        cost_estimate=pl.CostEstimate(flops=flops, bytes_accessed=1024, transcendentals=0),
    )(*args)


def tree(parts):
    if len(parts) == 1:
        return parts[0]
    if len(parts) == 2:
        return parts[0] + parts[1]
    return (parts[0] + parts[1]) + (parts[2] + parts[3])


def lane_total(value):
    return jnp.broadcast_to(jnp.sum(value, axis=1, keepdims=True), (value.shape[0], LANES))


def pack_norm(value):
    high = value.astype(BF16).astype(F32)
    rest = value - high
    middle = rest.astype(BF16).astype(F32)
    lane = lax.broadcasted_iota(jnp.int32, value.shape, 1)
    zero = jnp.zeros_like(value)
    return jnp.where(
        lane == 0, high, jnp.where(lane == 1, middle, jnp.where(lane == 2, rest - middle, zero))
    ).astype(BF16)


def unpack_norm(block):
    return lane_total(block.astype(F32))


def split(value, out_ref):
    scen = value.shape[0]
    high = value.astype(BF16)
    out_ref[:scen, :] = high
    out_ref[scen:, :] = (value - high.astype(F32)).astype(BF16)


def load_kernel(chunk, op_hbm, start_hbm, op_ref, image_ref, start_ref, sems):
    pieces = op_ref.shape[1] // chunk
    copies = [pltpu.make_async_copy(start_hbm, start_ref, sems.at[pieces])]
    for k in range(pieces):
        at = pl.ds(k * chunk, chunk)
        copies.append(pltpu.make_async_copy(op_hbm.at[:, at], op_ref.at[:, at], sems.at[k]))
    for copy in copies:
        copy.start()
    copies[0].wait()
    total = jnp.zeros(image_ref.shape, F32)
    for k in range(pieces):
        copies[k + 1].wait()
        at = pl.ds(k * chunk, chunk)
        total += lax.dot_general(
            start_ref[:, at].astype(BF16), op_ref[:, at], (((1,), (1,)), ((), ())), preferred_element_type=F32
        )
    image_ref[...] = total


def load(operator, start):
    rows, columns = operator.shape
    chunk = min(2048, columns)
    return call(
        functools.partial(load_kernel, chunk),
        (shape(rows, columns, dtype=BF16), shape(start.shape[0], rows)),
        (operator, start),
        [ANY, ANY],
        [pltpu.VMEM(start.shape, F32), pltpu.SemaphoreType.DMA((columns // chunk + 1,))],
    )


def place(near, distance):
    return (lax.axis_index("obs") & (near - 1)) ^ distance


def backward_kernel(near, distance, chunk, op_ref, w_ref, *refs):
    out_ref = refs[-1]
    scen = out_ref.shape[0]
    width = out_ref.shape[1] - LANES * (len(refs) - 1)
    w = w_ref[...]
    base = place(near, distance) * width
    for k in range(width // chunk):
        at = pl.ds(pl.multiple_of(base + k * chunk, chunk), chunk)
        both = jnp.dot(w, op_ref[:, at], preferred_element_type=F32)
        out_ref[:, k * chunk : (k + 1) * chunk] = (both[:scen] + both[scen:]).astype(out_ref.dtype)
    for norm_ref in refs[:-1]:
        out_ref[:, width:] = norm_ref[...]


def backward(near, distance, op, w, *norm):
    width = op.shape[1] // near
    scen = w.shape[0] // 2
    out = shape(scen, width + LANES, dtype=BF16) if norm else shape(scen, width)
    return call(
        functools.partial(backward_kernel, near, distance, min(1024, width)),
        out,
        (op, w, *norm),
    )


def forward_kernel(near, distance, op_ref, v_ref, *refs):
    out_ref = refs[-1]
    width = v_ref.shape[1]
    rows = op_ref.shape[0]
    v = v_ref[...]
    at = pl.ds(pl.multiple_of(place(near, distance) * width, width), width)
    image = lax.dot_general(v, op_ref[:, at], (((1,), (1,)), ((), ())), preferred_element_type=F32)
    wide = v.astype(F32)
    square = wide * wide
    norm = square[:, :LANES]
    for k in range(1, width // LANES):
        norm += square[:, k * LANES : (k + 1) * LANES]
    for sum_ref in refs[:-1]:
        image += sum_ref[:, :rows]
        norm += sum_ref[:, rows:]
    out_ref[:, :rows] = image
    out_ref[:, rows:] = norm


def forward(near, distance, op, v, *total):
    scen, width = v.shape
    rows = op.shape[0]
    return call(
        functools.partial(forward_kernel, near, distance),
        shape(scen, rows + LANES),
        (op, v, *total),
    )


def first_kernel(targets_ref, *refs):
    *part_refs, residual_ref, w_ref, norm_ref, packed_ref = refs
    residual = targets_ref[...] - tree([ref[...] for ref in part_refs])
    residual_ref[...] = residual
    norm_ref[...] = jnp.zeros(norm_ref.shape, F32)
    packed_ref[...] = jnp.zeros(packed_ref.shape, BF16)
    split(residual, w_ref)


def image_kernel(later, last, *refs):
    outs = 4 + (not last) * 2
    ins, (image_ref, gamma_ref, beta_ref, norm_ref, *more_refs) = refs[:-outs], refs[-outs:]
    if later:
        old_ref, old_gamma_ref, *ins = ins
    total = tree([ref[...] for ref in ins])
    rows = image_ref.shape[1]
    image = total[:, :rows]
    gamma = lane_total(total[:, rows:])
    beta = jnp.zeros_like(gamma)
    if later:
        beta = gamma / old_gamma_ref[...]
        image += jnp.concatenate([beta] * (rows // LANES), axis=1) * old_ref[...]
    image_ref[...] = image
    gamma_ref[...] = gamma
    beta_ref[...] = beta
    norm = lane_total(image * image)
    norm_ref[...] = norm
    if not last:
        packed_ref, w_ref = more_refs
        packed_ref[...] = pack_norm(norm)
        split(image, w_ref)


def add_kernel(sum_ref, got_ref, out_ref):
    out_ref[...] = sum_ref[...] + got_ref[:, : out_ref.shape[1]].astype(F32)


def near_kernel(order, sum_ref, norm_ref, *refs):
    *got_refs, out_ref = refs
    width = sum_ref.shape[1]
    total = sum_ref[...] + got_refs[-1][:, :width].astype(F32)
    norm = tree([norm_ref[...]] + [unpack_norm(ref[:, width:]) for _, ref in sorted(zip(order, got_refs), key=lambda pair: pair[0])])
    out_ref[:, :width] = total.astype(BF16)
    out_ref[:, width:] = pack_norm(norm)


def far_kernel(*refs):
    *got_refs, out_ref = refs
    width = out_ref.shape[1] - LANES
    out_ref[:, :width] = tree([ref[:, :width].astype(F32) for ref in got_refs]).astype(BF16)
    out_ref[:, width:] = pack_norm(tree([unpack_norm(ref[:, width:]) for ref in got_refs]))


def gradient_kernel(later, *refs):
    *ins, gradient_ref, rounded_ref, alpha_ref = refs
    if later:
        old_ref, gamma_ref, *ins = ins
    width = gradient_ref.shape[1]
    total = tree([ref[:, :width].astype(F32) for ref in ins])
    if later:
        alpha = gamma_ref[...] / tree([unpack_norm(ref[:, width:]) for ref in ins])
        alpha_ref[...] = alpha
        total = old_ref[...] - jnp.concatenate([alpha] * (width // LANES), axis=1) * total
    else:
        alpha_ref[...] = jnp.zeros(alpha_ref.shape, F32)
    gradient_ref[...] = total
    rounded_ref[...] = total.astype(BF16)


def directions_kernel(near, width, start_ref, *refs):
    *ins, direction_ref, solution_ref = refs
    alphas = ins[: ITERS - 1]
    betas = ins[ITERS - 1 : 2 * ITERS - 1]
    pieces = ins[2 * ITERS - 1 :]
    for d in range(near):
        base = place(near, d) * width
        for k in range(width // LANES):
            at = pl.ds(pl.multiple_of(base + k * LANES, LANES), LANES)
            here = slice(k * LANES, (k + 1) * LANES)
            solution = start_ref[:, at]
            direction = pieces[d][:, here].astype(F32)
            for index in range(1, ITERS):
                solution += alphas[index - 1][...] * direction
                direction = pieces[index * near + d][:, here].astype(F32) + betas[index][...] * direction
            direction_ref[:, at] = direction
            solution_ref[:, at] = solution


def last_kernel(parts, gamma_ref, direction_ref, base_ref, residual_ref, *refs):
    *ins, out_ref, out_residual_ref = refs
    norms = ins[:parts]
    alphas = ins[parts : parts + ITERS - 1]
    images = ins[parts + ITERS - 1 :]
    alpha = gamma_ref[...] / tree([ref[...] for ref in norms])

    def step(k, _):
        at = pl.ds(pl.multiple_of(k * LANES, LANES), LANES)
        out_ref[:, at] = base_ref[:, at] + alpha * direction_ref[:, at]
        return 0

    lax.fori_loop(0, out_ref.shape[1] // LANES, step, 0, unroll=8)
    residual = residual_ref[...]
    rows = residual.shape[1]
    for index in range(ITERS):
        factor = alpha if index == ITERS - 1 else alphas[index][...]
        residual -= jnp.concatenate([factor] * (rows // LANES), axis=1) * images[index][...]
    out_residual_ref[...] = residual


def exchange(value, axis, size, distance):
    return lax.ppermute(value, axis, [(i, i ^ distance) for i in range(size)])


def stages(size, stride=1):
    found = []
    while stride < size:
        members = 4 if size // stride % 4 == 0 else 2
        found.append((stride, members))
        stride *= members
    return found


def exchanged(value, axis, size, stride, members):
    return [value] + [exchange(value, axis, size, k * stride) for k in range(1, members)]


def parts_over(value, axis, size):
    parts = [value]
    for stride, members in stages(size):
        parts = exchanged(tree(parts), axis, size, stride, members)
    return parts


def shards(n_obs, n_par, operator, targets, start):
    rows, columns = operator.shape
    scen = start.shape[0]
    near = 4 if n_obs % 4 == 0 else n_obs
    width = columns // near
    lanes = shape(scen, LANES)
    image_shape = shape(scen, rows)
    term_shape = shape(2 * scen, rows, dtype=BF16)

    def gradient_parts(w, norm, packed):
        order = (3, 1, 2) if near == 4 else tuple(range(1, near))
        got = {d: exchange(backward(near, d, op, w, packed), "obs", n_obs, d) for d in order}
        total = backward(near, 0, op, w)
        for d in order[:-1]:
            total = call(add_kernel, shape(scen, width), (total, got[d]), flops=ADD_FLOPS)
        both = shape(scen, width + LANES, dtype=BF16)
        value = call(functools.partial(near_kernel, order), both, (total, norm, *(got[d] for d in order)))
        parts = [value]
        for index, (stride, members) in enumerate(stages(n_obs, near)):
            if index:
                value = call(far_kernel, both, parts)
            parts = exchanged(value, "obs", n_obs, stride, members)
        return parts

    def image_parts(mine):
        got = {d: exchange(mine, "obs", n_obs, d) for d in range(1, near)}
        total = forward(near, 0, op, mine)
        for d in got:
            total = forward(near, d, op, got[d], total)
        return parts_over(total, "par", n_par), [mine] + [got[d] for d in range(1, near)]

    op, first = load(operator, start)
    packed_lanes = shape(scen, LANES, dtype=BF16)
    residual, w, norm, packed = call(
        first_kernel, (image_shape, term_shape, lanes, packed_lanes), (targets, *parts_over(first, "par", n_par))
    )
    images, alphas, betas, pieces = [], [], [], []
    gradient = gamma = None
    for index in range(ITERS):
        parts = gradient_parts(w, norm, packed)
        gradient, rounded, alpha = call(
            functools.partial(gradient_kernel, index > 0),
            (shape(scen, width), shape(scen, width, dtype=BF16), lanes),
            ((gradient, gamma) if index else ()) + tuple(parts),
        )
        alphas += [alpha] if index else []
        parts, got = image_parts(rounded)
        pieces += got
        last = index == ITERS - 1
        image, gamma, beta, norm, *more = call(
            functools.partial(image_kernel, index > 0, last),
            (image_shape, lanes, lanes, lanes) + (() if last else (packed_lanes, term_shape)),
            ((image, gamma) if index else ()) + tuple(parts),
        )
        if not last:
            packed, w = more
        images.append(image)
        betas.append(beta)

    norms = parts_over(norm, "obs", n_obs)
    direction, base = call(
        functools.partial(directions_kernel, near, width),
        (shape(scen, columns), shape(scen, columns)),
        (start, *alphas, *betas, *pieces),
    )
    return call(
        functools.partial(last_kernel, len(norms)),
        (shape(scen, columns), image_shape),
        (gamma, direction, base, residual, *norms, *alphas, *images),
    )


def solution(mesh):
    return jax.shard_map(
        functools.partial(shards, mesh.shape["obs"], mesh.shape["par"]),
        mesh=mesh,
        in_specs=(P("obs", "par"), P(None, "obs"), P(None, "par")),
        out_specs=(P(None, "par"), P(None, "obs")),
        check_vma=False,
    )
```

```python
import functools

import jax
import jax.numpy as jnp
from jax import lax
from jax.experimental import pallas as pl
from jax.experimental.pallas import tpu as pltpu
from jax.sharding import PartitionSpec as P

ITERS = 4
EARLY = 4
ADD_FLOPS = 1 << 28
LANES = 128
F32 = jnp.float32
BF16 = jnp.bfloat16
VMEM = pl.BlockSpec(memory_space=pltpu.VMEM)
ANY = pl.BlockSpec(memory_space=pl.ANY)


def shape(*sizes, dtype=F32):
    return jax.ShapeDtypeStruct(sizes, dtype)


def call(body, out, args, specs=None, scratch=(), flops=0, aliases=None, out_specs=None):
    return pl.pallas_call(
        body,
        out_shape=out,
        in_specs=specs if specs is not None else [VMEM] * len(args),
        out_specs=out_specs or jax.tree.map(lambda _: VMEM, out),
        input_output_aliases=aliases or {},
        scratch_shapes=scratch,
        compiler_params=pltpu.CompilerParams(vmem_limit_bytes=24 << 20),
        cost_estimate=pl.CostEstimate(flops=flops, bytes_accessed=1024, transcendentals=0),
    )(*args)


def tree(parts):
    if len(parts) == 1:
        return parts[0]
    half = len(parts) // 2
    return tree(parts[:half]) + tree(parts[half:])


def lane_total(value):
    return jnp.broadcast_to(jnp.sum(value, axis=1, keepdims=True), (value.shape[0], LANES))


def pack_norm(value):
    high = value.astype(BF16).astype(F32)
    rest = value - high
    middle = rest.astype(BF16).astype(F32)
    lane = lax.broadcasted_iota(jnp.int32, value.shape, 1)
    zero = jnp.zeros_like(value)
    return jnp.where(
        lane == 0, high, jnp.where(lane == 1, middle, jnp.where(lane == 2, rest - middle, zero))
    ).astype(BF16)


def unpack_norm(block):
    return lane_total(block.astype(F32))


def split(value, out_ref):
    scen = value.shape[0]
    high = value.astype(BF16)
    out_ref[:scen, :] = high
    out_ref[scen:, :] = (value - high.astype(F32)).astype(BF16)


def bring(chunk, first, last, op_hbm, op_ref, sems):
    copies = []
    for k in range(first, last):
        at = pl.ds(k * chunk, chunk)
        copies.append(pltpu.make_async_copy(op_hbm.at[:, at], op_ref.at[:, at], sems.at[k]))
        copies[-1].start()
    return copies


def early_kernel(chunk, last, op_hbm, op_ref, sems):
    for copy in bring(chunk, 0, last, op_hbm, op_ref, sems):
        copy.wait()


def load_kernel(chunk, first, last, op_hbm, start_ref, early_ref, op_ref, image_ref, sems):
    del early_ref
    copies = bring(chunk, first, last, op_hbm, op_ref, sems)
    total = jnp.zeros(image_ref.shape, F32)
    for k in range(last):
        if k >= first:
            copies[k - first].wait()
        at = pl.ds(k * chunk, chunk)
        total += lax.dot_general(
            start_ref[:, at].astype(BF16), op_ref[:, at], (((1,), (1,)), ((), ())), preferred_element_type=F32
        )
    image_ref[...] = total.astype(BF16)


def load(operator, start):
    rows, columns = operator.shape
    chunk = min(1024, columns)
    pieces = columns // chunk
    first = pieces * EARLY // 16
    whole = shape(rows, columns, dtype=BF16)
    sems = [pltpu.SemaphoreType.DMA((pieces,))]
    early = call(functools.partial(early_kernel, chunk, first), whole, (operator,), [ANY], sems)
    return call(
        functools.partial(load_kernel, chunk, first, pieces),
        (whole, shape(start.shape[0], rows, dtype=BF16)),
        (operator, start, early),
        [ANY, VMEM, VMEM],
        sems,
        aliases={2: 0},
    )


def place(n_obs, near, distance):
    me = lax.axis_index("obs")
    own = me & (near - 1)
    if mirrored(n_obs, near):
        own = own ^ (((me >> 2) & 1) << 1)
    return own ^ distance


def mirrored(n_obs, near):
    return n_obs == 2 * near and near == 4


def backward_kernel(n_obs, near, distance, chunk, op_ref, w_ref, *refs):
    out_ref = refs[-1]
    scen = out_ref.shape[0]
    width = out_ref.shape[1] - LANES * (len(refs) - 1)
    w = w_ref[...]
    base = place(n_obs, near, distance) * width
    for k in range(width // chunk):
        at = pl.ds(pl.multiple_of(base + k * chunk, chunk), chunk)
        both = jnp.dot(w, op_ref[:, at], preferred_element_type=F32)
        out_ref[:, k * chunk : (k + 1) * chunk] = (both[:scen] + both[scen:]).astype(out_ref.dtype)
    for norm_ref in refs[:-1]:
        out_ref[:, width:] = norm_ref[...]


def backward(n_obs, near, distance, op, w, *norm):
    width = op.shape[1] // near
    scen = w.shape[0] // 2
    out = shape(scen, width + LANES, dtype=BF16) if norm else shape(scen, width)
    return call(
        functools.partial(backward_kernel, n_obs, near, distance, min(1024, width)),
        out,
        (op, w, *norm),
    )


def forward_kernel(n_obs, near, distance, op_ref, v_ref, *refs):
    out_ref = refs[-1]
    width = v_ref.shape[1]
    rows = op_ref.shape[0]
    v = v_ref[...]
    at = pl.ds(pl.multiple_of(place(n_obs, near, distance) * width, width), width)
    image = lax.dot_general(v, op_ref[:, at], (((1,), (1,)), ((), ())), preferred_element_type=F32)
    wide = v.astype(F32)
    square = wide * wide
    norm = square[:, :LANES]
    for k in range(1, width // LANES):
        norm += square[:, k * LANES : (k + 1) * LANES]
    for sum_ref in refs[:-1]:
        image += sum_ref[:, :rows]
        norm += sum_ref[:, rows:]
    if out_ref.dtype == BF16:
        norm = pack_norm(lane_total(norm))
    out_ref[:, :rows] = image.astype(out_ref.dtype)
    out_ref[:, rows:] = norm


def forward(n_obs, near, distance, dtype, op, v, *total):
    scen, width = v.shape
    rows = op.shape[0]
    return call(
        functools.partial(forward_kernel, n_obs, near, distance),
        shape(scen, rows + LANES, dtype=dtype),
        (op, v, *total),
    )


def first_kernel(targets_ref, *refs):
    *part_refs, residual_ref, w_ref, norm_ref, packed_ref = refs
    residual = targets_ref[...] - tree([ref[...].astype(F32) for ref in part_refs])
    residual_ref[...] = residual
    norm_ref[...] = jnp.zeros(norm_ref.shape, F32)
    packed_ref[...] = jnp.zeros(packed_ref.shape, BF16)
    split(residual, w_ref)


def image_kernel(later, last, *refs):
    outs = 4 + (not last) * 2
    ins, (image_ref, gamma_ref, beta_ref, norm_ref, *more_refs) = refs[:-outs], refs[-outs:]
    if later:
        old_ref, old_gamma_ref, *ins = ins
    rows = image_ref.shape[1]
    image = tree([ref[:, :rows].astype(F32) for ref in ins])
    gamma = tree([unpack_norm(ref[:, rows:]) for ref in ins])
    beta = jnp.zeros_like(gamma)
    if later:
        beta = gamma / old_gamma_ref[...]
        image += jnp.concatenate([beta] * (rows // LANES), axis=1) * old_ref[...]
    image_ref[...] = image
    gamma_ref[...] = gamma
    beta_ref[...] = beta
    norm = lane_total(image * image)
    norm_ref[...] = norm
    if not last:
        packed_ref, w_ref = more_refs
        packed_ref[...] = pack_norm(norm)
        split(image, w_ref)


def add_kernel(sum_ref, got_ref, out_ref):
    out_ref[...] = sum_ref[...] + got_ref[:, : out_ref.shape[1]].astype(F32)


def near_kernel(order, sum_ref, norm_ref, *refs):
    *got_refs, out_ref = refs
    width = sum_ref.shape[1]
    total = sum_ref[...] + got_refs[-1][:, :width].astype(F32)
    norm = tree([norm_ref[...]] + [unpack_norm(ref[:, width:]) for _, ref in sorted(zip(order, got_refs), key=lambda pair: pair[0])])
    out_ref[:, :width] = total.astype(BF16)
    out_ref[:, width:] = pack_norm(norm)


def far_kernel(normed, *refs):
    *got_refs, out_ref = refs
    width = out_ref.shape[1] - normed * LANES
    out_ref[:, :width] = tree([ref[:, :width].astype(F32) for ref in got_refs]).astype(BF16)
    if normed:
        out_ref[:, width:] = pack_norm(tree([unpack_norm(ref[:, width:]) for ref in got_refs]))


def gradient_kernel(later, *refs):
    *ins, gradient_ref, rounded_ref, alpha_ref = refs
    if later:
        old_ref, gamma_ref, *ins = ins
    width = gradient_ref.shape[1]
    total = tree([ref[:, :width].astype(F32) for ref in ins])
    if later:
        alpha = gamma_ref[...] / tree([unpack_norm(ref[:, width:]) for ref in ins])
        alpha_ref[...] = alpha
        total = old_ref[...] - jnp.concatenate([alpha] * (width // LANES), axis=1) * total
    else:
        alpha_ref[...] = jnp.zeros(alpha_ref.shape, F32)
    gradient_ref[...] = total
    rounded_ref[...] = total.astype(BF16)


def directions_kernel(n_obs, near, width, start_ref, *refs):
    *ins, direction_ref, solution_ref = refs
    alphas = ins[: ITERS - 1]
    betas = ins[ITERS - 1 : 2 * ITERS - 1]
    pieces = ins[2 * ITERS - 1 :]
    for d in range(near):
        base = place(n_obs, near, d) * width
        for k in range(width // LANES):
            at = pl.ds(pl.multiple_of(base + k * LANES, LANES), LANES)
            here = slice(k * LANES, (k + 1) * LANES)
            solution = start_ref[:, at]
            direction = pieces[d][:, here].astype(F32)
            for index in range(1, ITERS):
                solution += alphas[index - 1][...] * direction
                direction = pieces[index * near + d][:, here].astype(F32) + betas[index][...] * direction
            direction_ref[:, at] = direction
            solution_ref[:, at] = solution


def last_kernel(parts, chunk, gamma_ref, direction_ref, base_ref, residual_ref, *refs):
    *ins, out_hbm, out_residual_ref, out_ref, sems = refs
    norms = ins[:parts]
    alphas = ins[parts : parts + ITERS - 1]
    images = ins[parts + ITERS - 1 :]
    alpha = gamma_ref[...] / tree([ref[...] for ref in norms])
    wide = jnp.concatenate([alpha] * (chunk // LANES), axis=1)
    copies = []
    for k in range(out_ref.shape[1] // chunk):
        at = pl.ds(k * chunk, chunk)
        out_ref[:, at] = base_ref[:, at] + wide * direction_ref[:, at]
        copies.append(pltpu.make_async_copy(out_ref.at[:, at], out_hbm.at[:, at], sems.at[k]))
        copies[-1].start()
    residual = residual_ref[...]
    rows = residual.shape[1]
    for index in range(ITERS):
        factor = alpha if index == ITERS - 1 else alphas[index][...]
        residual -= jnp.concatenate([factor] * (rows // LANES), axis=1) * images[index][...]
    out_residual_ref[...] = residual
    for copy in copies:
        copy.wait()


def exchange(value, axis, size, distance):
    return lax.ppermute(value, axis, [(i, i ^ distance) for i in range(size)])


def stages(size, stride=1):
    found = []
    while stride < size:
        members = 4 if size // stride % 4 == 0 else 2
        found.append((stride, members))
        stride *= members
    return found


def exchanged(value, axis, size, stride, members):
    return [value] + [exchange(value, axis, size, k * stride) for k in range(1, members)]


def parts_over(value, axis, size, normed):
    parts = [value]
    for index, (stride, members) in enumerate(stages(size)):
        if index:
            value = call(functools.partial(far_kernel, normed), jax.ShapeDtypeStruct(value.shape, BF16), parts)
        parts = exchanged(value, axis, size, stride, members)
    return parts


def norm_kernel(mine_ref, *refs):
    first_ref, *got_refs, out_ref = refs
    own = jnp.where((lax.axis_index("par") & 1) == 0, mine_ref[...], first_ref[...])
    out_ref[...] = tree([own] + [ref[...] for ref in got_refs])


def norm_parts(norm, n_obs, n_par):
    half = n_obs // 2
    got = []
    for k in range(half):
        pairs = []
        for at in range(n_obs):
            for member in range(n_par):
                there = at ^ (half + k if member % 2 or not k else k)
                pairs.append((at * n_par + member, there * n_par + member))
        got.append(lax.ppermute(norm, ("obs", "par"), pairs))
    return exchanged(call(norm_kernel, jax.ShapeDtypeStruct(norm.shape, F32), (norm, *got)), "par", n_par, 1, 2)


def shards(n_obs, n_par, operator, targets, start):
    rows, columns = operator.shape
    scen = start.shape[0]
    near = 4 if n_obs % 4 == 0 else n_obs
    width = columns // near
    lanes = shape(scen, LANES)
    image_shape = shape(scen, rows)
    term_shape = shape(2 * scen, rows, dtype=BF16)

    def gradient_parts(w, norm, packed):
        order = (3, 1, 2) if near == 4 else tuple(range(1, near))
        got = {d: exchange(backward(n_obs, near, d, op, w, packed), "obs", n_obs, d) for d in order}
        total = backward(n_obs, near, 0, op, w)
        for d in order[:-1]:
            total = call(add_kernel, shape(scen, width), (total, got[d]), flops=ADD_FLOPS)
        both = shape(scen, width + LANES, dtype=BF16)
        value = call(functools.partial(near_kernel, order), both, (total, norm, *(got[d] for d in order)))
        parts = [value]
        for index, (stride, members) in enumerate(stages(n_obs, near)):
            if index:
                value = call(functools.partial(far_kernel, True), both, parts)
            if mirrored(n_obs, near):
                stride += 2
            parts = exchanged(value, "obs", n_obs, stride, members)
        return parts

    def image_parts(mine):
        got = {d: exchange(mine, "obs", n_obs, d) for d in range(1, near)}
        total = forward(n_obs, near, 0, F32, op, mine)
        for d in got:
            total = forward(n_obs, near, d, BF16 if d == near - 1 else F32, op, got[d], total)
        return parts_over(total, "par", n_par, True), [mine] + [got[d] for d in range(1, near)]

    op, first = load(operator, start)
    packed_lanes = shape(scen, LANES, dtype=BF16)
    residual, w, norm, packed = call(
        first_kernel, (image_shape, term_shape, lanes, packed_lanes), (targets, *parts_over(first, "par", n_par, False))
    )
    images, alphas, betas, pieces = [], [], [], []
    gradient = gamma = None
    for index in range(ITERS):
        parts = gradient_parts(w, norm, packed)
        gradient, rounded, alpha = call(
            functools.partial(gradient_kernel, index > 0),
            (shape(scen, width), shape(scen, width, dtype=BF16), lanes),
            ((gradient, gamma) if index else ()) + tuple(parts),
        )
        alphas += [alpha] if index else []
        parts, got = image_parts(rounded)
        pieces += got
        last = index == ITERS - 1
        image, gamma, beta, norm, *more = call(
            functools.partial(image_kernel, index > 0, last),
            (image_shape, lanes, lanes, lanes) + (() if last else (packed_lanes, term_shape)),
            ((image, gamma) if index else ()) + tuple(parts),
        )
        if not last:
            packed, w = more
        images.append(image)
        betas.append(beta)

    norms = norm_parts(norm, n_obs, n_par)
    direction, base = call(
        functools.partial(directions_kernel, n_obs, near, width),
        (shape(scen, columns), shape(scen, columns)),
        (start, *alphas, *betas, *pieces),
    )
    chunk = min(2048, columns)
    return call(
        functools.partial(last_kernel, len(norms), chunk),
        (shape(scen, columns), image_shape),
        (gamma, direction, base, residual, *norms, *alphas, *images),
        scratch=[pltpu.VMEM((scen, columns), F32), pltpu.SemaphoreType.DMA((columns // chunk,))],
        out_specs=(ANY, VMEM),
    )


def solution(mesh):
    return jax.shard_map(
        functools.partial(shards, mesh.shape["obs"], mesh.shape["par"]),
        mesh=mesh,
        in_specs=(P("obs", "par"), P(None, "obs"), P(None, "par")),
        out_specs=(P(None, "par"), P(None, "obs")),
        check_vma=False,
    )
```

```python
import functools

import jax
import jax.numpy as jnp
from jax import lax
from jax.experimental import pallas as pl
from jax.experimental.pallas import tpu as pltpu
from jax.sharding import PartitionSpec as P

ITERS = 4
EARLY = 4
ADD_FLOPS = 1 << 28
LANES = 128
F32 = jnp.float32
BF16 = jnp.bfloat16
VMEM = pl.BlockSpec(memory_space=pltpu.VMEM)
ANY = pl.BlockSpec(memory_space=pl.ANY)


def shape(*sizes, dtype=F32):
    return jax.ShapeDtypeStruct(sizes, dtype)


def call(body, out, args, specs=None, scratch=(), flops=0, aliases=None, out_specs=None):
    return pl.pallas_call(
        body,
        out_shape=out,
        in_specs=specs if specs is not None else [VMEM] * len(args),
        out_specs=out_specs or jax.tree.map(lambda _: VMEM, out),
        input_output_aliases=aliases or {},
        scratch_shapes=scratch,
        compiler_params=pltpu.CompilerParams(vmem_limit_bytes=24 << 20),
        cost_estimate=pl.CostEstimate(flops=flops, bytes_accessed=1024, transcendentals=0),
    )(*args)


def tree(parts):
    if len(parts) == 1:
        return parts[0]
    half = len(parts) // 2
    return tree(parts[:half]) + tree(parts[half:])


def lane_total(value):
    return jnp.broadcast_to(jnp.sum(value, axis=1, keepdims=True), (value.shape[0], LANES))


def pack_norm(value):
    high = value.astype(BF16).astype(F32)
    rest = value - high
    middle = rest.astype(BF16).astype(F32)
    lane = lax.broadcasted_iota(jnp.int32, value.shape, 1)
    zero = jnp.zeros_like(value)
    return jnp.where(
        lane == 0, high, jnp.where(lane == 1, middle, jnp.where(lane == 2, rest - middle, zero))
    ).astype(BF16)


def unpack_norm(block):
    return lane_total(block.astype(F32))


def split(value, out_ref):
    scen = value.shape[0]
    high = value.astype(BF16)
    out_ref[:scen, :] = high
    out_ref[scen:, :] = (value - high.astype(F32)).astype(BF16)


def bring(chunk, first, last, op_hbm, op_ref, sems):
    copies = []
    for k in range(first, last):
        at = pl.ds(k * chunk, chunk)
        copies.append(pltpu.make_async_copy(op_hbm.at[:, at], op_ref.at[:, at], sems.at[k]))
        copies[-1].start()
    return copies


def early_kernel(chunk, last, op_hbm, op_ref, sems):
    for copy in bring(chunk, 0, last, op_hbm, op_ref, sems):
        copy.wait()


def load_kernel(chunk, first, last, op_hbm, start_ref, early_ref, op_ref, image_ref, sems):
    del early_ref
    copies = bring(chunk, first, last, op_hbm, op_ref, sems)
    total = jnp.zeros(image_ref.shape, F32)
    for k in range(last):
        if k >= first:
            copies[k - first].wait()
        at = pl.ds(k * chunk, chunk)
        total += lax.dot_general(
            start_ref[:, at].astype(BF16), op_ref[:, at], (((1,), (1,)), ((), ())), preferred_element_type=F32
        )
    image_ref[...] = total.astype(BF16)


def load(operator, start):
    rows, columns = operator.shape
    chunk = min(1024, columns)
    pieces = columns // chunk
    first = pieces * EARLY // 16
    whole = shape(rows, columns, dtype=BF16)
    sems = [pltpu.SemaphoreType.DMA((pieces,))]
    early = call(functools.partial(early_kernel, chunk, first), whole, (operator,), [ANY], sems)
    return call(
        functools.partial(load_kernel, chunk, first, pieces),
        (whole, shape(start.shape[0], rows, dtype=BF16)),
        (operator, start, early),
        [ANY, VMEM, VMEM],
        sems,
        aliases={2: 0},
    )


def place(n_obs, near, distance):
    me = lax.axis_index("obs")
    own = me & (near - 1)
    if mirrored(n_obs, near):
        own = own ^ (((me >> 2) & 1) << 1)
    return own ^ distance


def mirrored(n_obs, near):
    return n_obs == 2 * near and near == 4


def backward_kernel(n_obs, near, distance, chunk, op_ref, w_ref, *refs):
    out_ref = refs[-1]
    scen = out_ref.shape[0]
    width = out_ref.shape[1] - LANES * (len(refs) - 1)
    w = w_ref[...]
    base = place(n_obs, near, distance) * width
    for k in range(width // chunk):
        at = pl.ds(pl.multiple_of(base + k * chunk, chunk), chunk)
        both = jnp.dot(w, op_ref[:, at], preferred_element_type=F32)
        out_ref[:, k * chunk : (k + 1) * chunk] = (both[:scen] + both[scen:]).astype(out_ref.dtype)
    for norm_ref in refs[:-1]:
        out_ref[:, width:] = norm_ref[...]


def backward(n_obs, near, distance, op, w, *norm):
    width = op.shape[1] // near
    scen = w.shape[0] // 2
    out = shape(scen, width + LANES, dtype=BF16) if norm else shape(scen, width)
    return call(
        functools.partial(backward_kernel, n_obs, near, distance, min(1024, width)),
        out,
        (op, w, *norm),
    )


def forward_kernel(n_obs, near, distance, op_ref, v_ref, *refs):
    out_ref = refs[-1]
    width = v_ref.shape[1]
    rows = op_ref.shape[0]
    v = v_ref[...]
    at = pl.ds(pl.multiple_of(place(n_obs, near, distance) * width, width), width)
    image = lax.dot_general(v, op_ref[:, at], (((1,), (1,)), ((), ())), preferred_element_type=F32)
    wide = v.astype(F32)
    square = wide * wide
    norm = square[:, :LANES]
    for k in range(1, width // LANES):
        norm += square[:, k * LANES : (k + 1) * LANES]
    for sum_ref in refs[:-1]:
        image += sum_ref[:, :rows]
        norm += sum_ref[:, rows:]
    if out_ref.dtype == BF16:
        norm = pack_norm(lane_total(norm))
    out_ref[:, :rows] = image.astype(out_ref.dtype)
    out_ref[:, rows:] = norm


def forward(n_obs, near, distance, dtype, op, v, *total):
    scen, width = v.shape
    rows = op.shape[0]
    return call(
        functools.partial(forward_kernel, n_obs, near, distance),
        shape(scen, rows + LANES, dtype=dtype),
        (op, v, *total),
    )


def first_kernel(targets_ref, *refs):
    *part_refs, residual_ref, w_ref, norm_ref, packed_ref = refs
    residual = targets_ref[...] - tree([ref[...].astype(F32) for ref in part_refs])
    residual_ref[...] = residual
    norm_ref[...] = jnp.zeros(norm_ref.shape, F32)
    packed_ref[...] = jnp.zeros(packed_ref.shape, BF16)
    split(residual, w_ref)


def image_kernel(later, last, *refs):
    outs = 4 + (not last) * 2
    ins, (image_ref, gamma_ref, beta_ref, norm_ref, *more_refs) = refs[:-outs], refs[-outs:]
    if later:
        old_ref, old_gamma_ref, *ins = ins
    rows = image_ref.shape[1]
    image = tree([ref[:, :rows].astype(F32) for ref in ins])
    gamma = tree([unpack_norm(ref[:, rows:]) for ref in ins])
    beta = jnp.zeros_like(gamma)
    if later:
        beta = gamma / old_gamma_ref[...]
        image += jnp.concatenate([beta] * (rows // LANES), axis=1) * old_ref[...]
    image_ref[...] = image
    gamma_ref[...] = gamma
    beta_ref[...] = beta
    norm = lane_total(image * image)
    norm_ref[...] = norm
    if not last:
        packed_ref, w_ref = more_refs
        packed_ref[...] = pack_norm(norm)
        split(image, w_ref)


def add_kernel(sum_ref, got_ref, out_ref):
    out_ref[...] = sum_ref[...] + got_ref[:, : out_ref.shape[1]].astype(F32)


def near_kernel(order, sum_ref, norm_ref, *refs):
    *got_refs, out_ref = refs
    width = sum_ref.shape[1]
    total = sum_ref[...] + got_refs[-1][:, :width].astype(F32)
    norm = tree([norm_ref[...]] + [unpack_norm(ref[:, width:]) for _, ref in sorted(zip(order, got_refs), key=lambda pair: pair[0])])
    out_ref[:, :width] = total.astype(BF16)
    out_ref[:, width:] = pack_norm(norm)


def far_kernel(normed, *refs):
    *got_refs, out_ref = refs
    width = out_ref.shape[1] - normed * LANES
    out_ref[:, :width] = tree([ref[:, :width].astype(F32) for ref in got_refs]).astype(BF16)
    if normed:
        out_ref[:, width:] = pack_norm(tree([unpack_norm(ref[:, width:]) for ref in got_refs]))


def gradient_kernel(later, *refs):
    *ins, gradient_ref, rounded_ref, alpha_ref = refs
    if later:
        old_ref, gamma_ref, *ins = ins
    width = gradient_ref.shape[1]
    total = tree([ref[:, :width].astype(F32) for ref in ins])
    if later:
        alpha = gamma_ref[...] / tree([unpack_norm(ref[:, width:]) for ref in ins])
        alpha_ref[...] = alpha
        total = old_ref[...] - jnp.concatenate([alpha] * (width // LANES), axis=1) * total
    else:
        alpha_ref[...] = jnp.zeros(alpha_ref.shape, F32)
    gradient_ref[...] = total
    rounded_ref[...] = total.astype(BF16)


def directions_kernel(n_obs, near, width, start_ref, *refs):
    *ins, direction_ref, solution_ref = refs
    alphas = ins[: ITERS - 1]
    betas = ins[ITERS - 1 : 2 * ITERS - 1]
    pieces = ins[2 * ITERS - 1 :]
    for d in range(near):
        base = place(n_obs, near, d) * width
        for k in range(width // LANES):
            at = pl.ds(pl.multiple_of(base + k * LANES, LANES), LANES)
            here = slice(k * LANES, (k + 1) * LANES)
            solution = start_ref[:, at]
            direction = pieces[d][:, here].astype(F32)
            for index in range(1, ITERS):
                solution += alphas[index - 1][...] * direction
                direction = pieces[index * near + d][:, here].astype(F32) + betas[index][...] * direction
            direction_ref[:, at] = direction
            solution_ref[:, at] = solution


def last_kernel(parts, chunk, gamma_ref, direction_ref, base_ref, residual_ref, *refs):
    *ins, out_hbm, out_residual_ref, out_ref, sems = refs
    norms = ins[:parts]
    alphas = ins[parts : parts + ITERS - 1]
    images = ins[parts + ITERS - 1 :]
    alpha = gamma_ref[...] / tree([ref[...] for ref in norms])
    wide = jnp.concatenate([alpha] * (chunk // LANES), axis=1)
    copies = []
    for k in range(out_ref.shape[1] // chunk):
        at = pl.ds(k * chunk, chunk)
        out_ref[:, at] = base_ref[:, at] + wide * direction_ref[:, at]
        copies.append(pltpu.make_async_copy(out_ref.at[:, at], out_hbm.at[:, at], sems.at[k]))
        copies[-1].start()
    residual = residual_ref[...]
    rows = residual.shape[1]
    for index in range(ITERS):
        factor = alpha if index == ITERS - 1 else alphas[index][...]
        residual -= jnp.concatenate([factor] * (rows // LANES), axis=1) * images[index][...]
    out_residual_ref[...] = residual
    for copy in copies:
        copy.wait()


def exchange(value, axis, size, distance):
    return lax.ppermute(value, axis, [(i, i ^ distance) for i in range(size)])


def stages(size, stride=1):
    found = []
    while stride < size:
        members = 4 if size // stride % 4 == 0 else 2
        found.append((stride, members))
        stride *= members
    return found


def exchanged(value, axis, size, stride, members):
    return [value] + [exchange(value, axis, size, k * stride) for k in range(1, members)]


def parts_over(value, axis, size, normed):
    parts = [value]
    for index, (stride, members) in enumerate(stages(size)):
        if index:
            value = call(functools.partial(far_kernel, normed), jax.ShapeDtypeStruct(value.shape, BF16), parts)
        parts = exchanged(value, axis, size, stride, members)
    return parts


def norm_kernel(mine_ref, *refs):
    first_ref, *got_refs, out_ref = refs
    own = jnp.where((lax.axis_index("par") & 1) == 0, mine_ref[...], first_ref[...])
    out_ref[...] = tree([own] + [ref[...] for ref in got_refs])


def norm_parts(norm, n_obs, n_par):
    half = n_obs // 2
    got = []
    for k in range(half):
        pairs = []
        for at in range(n_obs):
            for member in range(n_par):
                there = at ^ (half + k if member % 2 or not k else k)
                pairs.append((at * n_par + member, there * n_par + member))
        got.append(lax.ppermute(norm, ("obs", "par"), pairs))
    return exchanged(call(norm_kernel, jax.ShapeDtypeStruct(norm.shape, F32), (norm, *got)), "par", n_par, 1, 2)


def shards(n_obs, n_par, operator, targets, start):
    rows, columns = operator.shape
    scen = start.shape[0]
    near = 4 if n_obs % 4 == 0 else n_obs
    width = columns // near
    lanes = shape(scen, LANES)
    image_shape = shape(scen, rows)
    term_shape = shape(2 * scen, rows, dtype=BF16)

    def gradient_parts(w, norm, packed):
        order = (2, 1, 3) if near == 4 else tuple(range(1, near))
        got = {d: exchange(backward(n_obs, near, d, op, w, packed), "obs", n_obs, d) for d in order}
        total = backward(n_obs, near, 0, op, w)
        for d in order[:-1]:
            total = call(add_kernel, shape(scen, width), (total, got[d]), flops=ADD_FLOPS)
        both = shape(scen, width + LANES, dtype=BF16)
        value = call(functools.partial(near_kernel, order), both, (total, norm, *(got[d] for d in order)))
        parts = [value]
        for index, (stride, members) in enumerate(stages(n_obs, near)):
            if index:
                value = call(functools.partial(far_kernel, True), both, parts)
            if mirrored(n_obs, near):
                stride += 2
            parts = exchanged(value, "obs", n_obs, stride, members)
        return parts

    def image_parts(mine):
        got = {d: exchange(mine, "obs", n_obs, d) for d in range(1, near)}
        total = forward(n_obs, near, 0, F32, op, mine)
        for d in got:
            total = forward(n_obs, near, d, BF16 if d == near - 1 else F32, op, got[d], total)
        return parts_over(total, "par", n_par, True), [mine] + [got[d] for d in range(1, near)]

    op, first = load(operator, start)
    packed_lanes = shape(scen, LANES, dtype=BF16)
    residual, w, norm, packed = call(
        first_kernel, (image_shape, term_shape, lanes, packed_lanes), (targets, *parts_over(first, "par", n_par, False))
    )
    images, alphas, betas, pieces = [], [], [], []
    gradient = gamma = None
    for index in range(ITERS):
        parts = gradient_parts(w, norm, packed)
        gradient, rounded, alpha = call(
            functools.partial(gradient_kernel, index > 0),
            (shape(scen, width), shape(scen, width, dtype=BF16), lanes),
            ((gradient, gamma) if index else ()) + tuple(parts),
        )
        alphas += [alpha] if index else []
        parts, got = image_parts(rounded)
        pieces += got
        last = index == ITERS - 1
        image, gamma, beta, norm, *more = call(
            functools.partial(image_kernel, index > 0, last),
            (image_shape, lanes, lanes, lanes) + (() if last else (packed_lanes, term_shape)),
            ((image, gamma) if index else ()) + tuple(parts),
        )
        if not last:
            packed, w = more
        images.append(image)
        betas.append(beta)

    norms = norm_parts(norm, n_obs, n_par)
    direction, base = call(
        functools.partial(directions_kernel, n_obs, near, width),
        (shape(scen, columns), shape(scen, columns)),
        (start, *alphas, *betas, *pieces),
    )
    chunk = min(2048, columns)
    return call(
        functools.partial(last_kernel, len(norms), chunk),
        (shape(scen, columns), image_shape),
        (gamma, direction, base, residual, *norms, *alphas, *images),
        scratch=[pltpu.VMEM((scen, columns), F32), pltpu.SemaphoreType.DMA((columns // chunk,))],
        out_specs=(ANY, VMEM),
    )


def solution(mesh):
    return jax.shard_map(
        functools.partial(shards, mesh.shape["obs"], mesh.shape["par"]),
        mesh=mesh,
        in_specs=(P("obs", "par"), P(None, "obs"), P(None, "par")),
        out_specs=(P(None, "par"), P(None, "obs")),
        check_vma=False,
    )
```

```python
import functools

import jax
import jax.numpy as jnp
from jax import lax
from jax.experimental import pallas as pl
from jax.experimental.pallas import tpu as pltpu
from jax.sharding import PartitionSpec as P

ITERS = 4
EARLY = 4
LIMIT = 8
ADD_FLOPS = 1 << 28
LANES = 128
F32 = jnp.float32
BF16 = jnp.bfloat16
VMEM = pl.BlockSpec(memory_space=pltpu.VMEM)
ANY = pl.BlockSpec(memory_space=pl.ANY)


def shape(*sizes, dtype=F32):
    return jax.ShapeDtypeStruct(sizes, dtype)


def call(body, out, args, specs=None, scratch=(), flops=0, aliases=None, out_specs=None, limit=LIMIT):
    return pl.pallas_call(
        body,
        out_shape=out,
        in_specs=specs if specs is not None else [VMEM] * len(args),
        out_specs=out_specs or jax.tree.map(lambda _: VMEM, out),
        input_output_aliases=aliases or {},
        scratch_shapes=scratch,
        compiler_params=pltpu.CompilerParams(vmem_limit_bytes=limit << 20),
        cost_estimate=pl.CostEstimate(flops=flops, bytes_accessed=1024, transcendentals=0),
    )(*args)


def tree(parts):
    if len(parts) == 1:
        return parts[0]
    half = len(parts) // 2
    return tree(parts[:half]) + tree(parts[half:])


def lane_total(value):
    return jnp.broadcast_to(jnp.sum(value, axis=1, keepdims=True), (value.shape[0], LANES))


def pack_norm(value):
    high = value.astype(BF16).astype(F32)
    rest = value - high
    middle = rest.astype(BF16).astype(F32)
    lane = lax.broadcasted_iota(jnp.int32, value.shape, 1)
    zero = jnp.zeros_like(value)
    return jnp.where(
        lane == 0, high, jnp.where(lane == 1, middle, jnp.where(lane == 2, rest - middle, zero))
    ).astype(BF16)


def unpack_norm(block):
    return lane_total(block.astype(F32))


def split(value, out_ref):
    scen = value.shape[0]
    high = value.astype(BF16)
    out_ref[:scen, :] = high
    out_ref[scen:, :] = (value - high.astype(F32)).astype(BF16)


def bring(chunk, first, last, op_hbm, op_ref, sems):
    copies = []
    for k in range(first, last):
        at = pl.ds(k * chunk, chunk)
        copies.append(pltpu.make_async_copy(op_hbm.at[:, at], op_ref.at[:, at], sems.at[k]))
        copies[-1].start()
    return copies


def early_kernel(chunk, last, op_hbm, op_ref, sems):
    for copy in bring(chunk, 0, last, op_hbm, op_ref, sems):
        copy.wait()


def load_kernel(chunk, first, last, op_hbm, start_ref, early_ref, op_ref, image_ref, sems):
    del early_ref
    copies = bring(chunk, first, last, op_hbm, op_ref, sems)
    total = jnp.zeros(image_ref.shape, F32)
    for k in range(last):
        if k >= first:
            copies[k - first].wait()
        at = pl.ds(k * chunk, chunk)
        total += lax.dot_general(
            start_ref[:, at].astype(BF16), op_ref[:, at], (((1,), (1,)), ((), ())), preferred_element_type=F32
        )
    image_ref[...] = total.astype(BF16)


def load(operator, start):
    rows, columns = operator.shape
    chunk = min(1024, columns)
    pieces = columns // chunk
    first = pieces * EARLY // 16
    whole = shape(rows, columns, dtype=BF16)
    sems = [pltpu.SemaphoreType.DMA((pieces,))]
    early = call(functools.partial(early_kernel, chunk, first), whole, (operator,), [ANY], sems, limit=24)
    return call(
        functools.partial(load_kernel, chunk, first, pieces),
        (whole, shape(start.shape[0], rows, dtype=BF16)),
        (operator, start, early),
        [ANY, VMEM, VMEM],
        sems,
        aliases={2: 0},
        limit=24,
    )


def place(n_obs, near, distance):
    me = lax.axis_index("obs")
    own = me & (near - 1)
    if mirrored(n_obs, near):
        own = own ^ (((me >> 2) & 1) << 1)
    return own ^ distance


def mirrored(n_obs, near):
    return n_obs == 2 * near and near == 4


def backward_kernel(n_obs, near, distance, chunk, op_ref, w_ref, *refs):
    out_ref = refs[-1]
    scen = out_ref.shape[0]
    width = out_ref.shape[1] - LANES * (len(refs) - 1)
    w = w_ref[...]
    base = place(n_obs, near, distance) * width
    for k in range(width // chunk):
        at = pl.ds(pl.multiple_of(base + k * chunk, chunk), chunk)
        both = jnp.dot(w, op_ref[:, at], preferred_element_type=F32)
        out_ref[:, k * chunk : (k + 1) * chunk] = (both[:scen] + both[scen:]).astype(out_ref.dtype)
    for norm_ref in refs[:-1]:
        out_ref[:, width:] = norm_ref[...]


def backward(n_obs, near, distance, op, w, *norm):
    width = op.shape[1] // near
    scen = w.shape[0] // 2
    out = shape(scen, width + LANES, dtype=BF16) if norm else shape(scen, width)
    return call(
        functools.partial(backward_kernel, n_obs, near, distance, min(1024, width)),
        out,
        (op, w, *norm),
    )


def turn_kernel(n_obs, near, distance, op_ref, out_ref):
    width = out_ref.shape[0]
    chunk = min(512, width)
    base = place(n_obs, near, distance) * width
    for first in range(0, width, chunk):
        at = pl.ds(pl.multiple_of(base + first, chunk), chunk)
        out_ref[first : first + chunk, :] = op_ref[:, at].T


def turn(n_obs, near, distance, op):
    rows, columns = op.shape
    return call(
        functools.partial(turn_kernel, n_obs, near, distance), shape(columns // near, rows, dtype=BF16), (op,)
    )


def forward_kernel(turned_ref, v_ref, *refs):
    out_ref = refs[-1]
    width, rows = turned_ref.shape
    v = v_ref[...]
    image = jnp.dot(v, turned_ref[...], preferred_element_type=F32)
    wide = v.astype(F32)
    square = wide * wide
    norm = square[:, :LANES]
    for k in range(1, width // LANES):
        norm += square[:, k * LANES : (k + 1) * LANES]
    for sum_ref in refs[:-1]:
        image += sum_ref[:, :rows]
        norm += sum_ref[:, rows:]
    if out_ref.dtype == BF16:
        norm = pack_norm(lane_total(norm))
    out_ref[:, :rows] = image.astype(out_ref.dtype)
    out_ref[:, rows:] = norm


def forward(dtype, turned, v, *total):
    return call(
        forward_kernel, shape(v.shape[0], turned.shape[1] + LANES, dtype=dtype), (turned, v, *total)
    )


def first_kernel(targets_ref, *refs):
    *part_refs, residual_ref, w_ref, norm_ref, packed_ref = refs
    residual = targets_ref[...] - tree([ref[...].astype(F32) for ref in part_refs])
    residual_ref[...] = residual
    norm_ref[...] = jnp.zeros(norm_ref.shape, F32)
    packed_ref[...] = jnp.zeros(packed_ref.shape, BF16)
    split(residual, w_ref)


def image_kernel(later, last, *refs):
    outs = 4 + (not last) * 2
    ins, (image_ref, gamma_ref, beta_ref, norm_ref, *more_refs) = refs[:-outs], refs[-outs:]
    if later:
        old_ref, old_gamma_ref, *ins = ins
    rows = image_ref.shape[1]
    image = tree([ref[:, :rows].astype(F32) for ref in ins])
    gamma = tree([unpack_norm(ref[:, rows:]) for ref in ins])
    beta = jnp.zeros_like(gamma)
    if later:
        beta = gamma / old_gamma_ref[...]
        image += jnp.concatenate([beta] * (rows // LANES), axis=1) * old_ref[...]
    image_ref[...] = image
    gamma_ref[...] = gamma
    beta_ref[...] = beta
    norm = lane_total(image * image)
    norm_ref[...] = norm
    if not last:
        packed_ref, w_ref = more_refs
        packed_ref[...] = pack_norm(norm)
        split(image, w_ref)


def add_kernel(sum_ref, got_ref, out_ref):
    out_ref[...] = sum_ref[...] + got_ref[:, : out_ref.shape[1]].astype(F32)


def near_kernel(order, sum_ref, norm_ref, *refs):
    *got_refs, out_ref = refs
    width = sum_ref.shape[1]
    total = sum_ref[...] + got_refs[-1][:, :width].astype(F32)
    norm = tree([norm_ref[...]] + [unpack_norm(ref[:, width:]) for _, ref in sorted(zip(order, got_refs), key=lambda pair: pair[0])])
    out_ref[:, :width] = total.astype(BF16)
    out_ref[:, width:] = pack_norm(norm)


def far_kernel(normed, *refs):
    *got_refs, out_ref = refs
    width = out_ref.shape[1] - normed * LANES
    out_ref[:, :width] = tree([ref[:, :width].astype(F32) for ref in got_refs]).astype(BF16)
    if normed:
        out_ref[:, width:] = pack_norm(tree([unpack_norm(ref[:, width:]) for ref in got_refs]))


def gradient_kernel(later, before, *refs):
    *ins, gradient_ref, rounded_ref, alpha_ref = refs
    if not later:
        ins = ins[before:]
    if later:
        old_ref, gamma_ref, *ins = ins
    width = gradient_ref.shape[1]
    total = tree([ref[:, :width].astype(F32) for ref in ins])
    if later:
        alpha = gamma_ref[...] / tree([unpack_norm(ref[:, width:]) for ref in ins])
        alpha_ref[...] = alpha
        total = old_ref[...] - jnp.concatenate([alpha] * (width // LANES), axis=1) * total
    else:
        alpha_ref[...] = jnp.zeros(alpha_ref.shape, F32)
    gradient_ref[...] = total
    rounded_ref[...] = total.astype(BF16)


def directions_kernel(n_obs, near, width, start_ref, *refs):
    *ins, direction_ref, solution_ref = refs
    alphas = ins[: ITERS - 1]
    betas = ins[ITERS - 1 : 2 * ITERS - 1]
    pieces = ins[2 * ITERS - 1 :]
    for d in range(near):
        base = place(n_obs, near, d) * width
        for k in range(width // LANES):
            at = pl.ds(pl.multiple_of(base + k * LANES, LANES), LANES)
            here = slice(k * LANES, (k + 1) * LANES)
            solution = start_ref[:, at]
            direction = pieces[d][:, here].astype(F32)
            for index in range(1, ITERS):
                solution += alphas[index - 1][...] * direction
                direction = pieces[index * near + d][:, here].astype(F32) + betas[index][...] * direction
            direction_ref[:, at] = direction
            solution_ref[:, at] = solution


def last_kernel(parts, gamma_ref, direction_ref, base_ref, residual_ref, *refs):
    *ins, out_ref, out_residual_ref = refs
    norms = ins[:parts]
    alphas = ins[parts : parts + ITERS - 1]
    images = ins[parts + ITERS - 1 :]
    alpha = gamma_ref[...] / tree([ref[...] for ref in norms])

    def step(k, _):
        at = pl.ds(pl.multiple_of(k * LANES, LANES), LANES)
        out_ref[:, at] = base_ref[:, at] + alpha * direction_ref[:, at]
        return 0

    lax.fori_loop(0, out_ref.shape[1] // LANES, step, 0, unroll=8)
    residual = residual_ref[...]
    rows = residual.shape[1]
    for index in range(ITERS):
        factor = alpha if index == ITERS - 1 else alphas[index][...]
        residual -= jnp.concatenate([factor] * (rows // LANES), axis=1) * images[index][...]
    out_residual_ref[...] = residual


def exchange(value, axis, size, distance):
    return lax.ppermute(value, axis, [(i, i ^ distance) for i in range(size)])


def stages(size, stride=1):
    found = []
    while stride < size:
        members = 4 if size // stride % 4 == 0 else 2
        found.append((stride, members))
        stride *= members
    return found


def exchanged(value, axis, size, stride, members):
    return [value] + [exchange(value, axis, size, k * stride) for k in range(1, members)]


def parts_over(value, axis, size, normed):
    parts = [value]
    for index, (stride, members) in enumerate(stages(size)):
        if index:
            value = call(functools.partial(far_kernel, normed), jax.ShapeDtypeStruct(value.shape, BF16), parts)
        parts = exchanged(value, axis, size, stride, members)
    return parts


def norm_kernel(mine_ref, *refs):
    first_ref, *got_refs, out_ref = refs
    own = jnp.where((lax.axis_index("par") & 1) == 0, mine_ref[...], first_ref[...])
    out_ref[...] = tree([own] + [ref[...] for ref in got_refs])


def norm_parts(norm, n_obs, n_par):
    half = n_obs // 2
    got = []
    for k in range(half):
        pairs = []
        for at in range(n_obs):
            for member in range(n_par):
                there = at ^ (half + k if member % 2 or not k else k)
                pairs.append((at * n_par + member, there * n_par + member))
        got.append(lax.ppermute(norm, ("obs", "par"), pairs))
    return exchanged(call(norm_kernel, jax.ShapeDtypeStruct(norm.shape, F32), (norm, *got)), "par", n_par, 1, 2)


def shards(n_obs, n_par, operator, targets, start):
    rows, columns = operator.shape
    scen = start.shape[0]
    near = 4 if n_obs % 4 == 0 else n_obs
    width = columns // near
    lanes = shape(scen, LANES)
    image_shape = shape(scen, rows)
    term_shape = shape(2 * scen, rows, dtype=BF16)

    def gradient_parts(w, norm, packed):
        order = (2, 1, 3) if near == 4 else tuple(range(1, near))
        got = {d: exchange(backward(n_obs, near, d, op, w, packed), "obs", n_obs, d) for d in order}
        total = backward(n_obs, near, 0, op, w)
        for d in order[:-1]:
            total = call(add_kernel, shape(scen, width), (total, got[d]), flops=ADD_FLOPS)
        both = shape(scen, width + LANES, dtype=BF16)
        value = call(functools.partial(near_kernel, order), both, (total, norm, *(got[d] for d in order)))
        parts = [value]
        for index, (stride, members) in enumerate(stages(n_obs, near)):
            if index:
                value = call(functools.partial(far_kernel, True), both, parts)
            if mirrored(n_obs, near):
                stride += 2
            parts = exchanged(value, "obs", n_obs, stride, members)
        return parts

    def image_parts(mine):
        got = {d: exchange(mine, "obs", n_obs, d) for d in range(1, near)}
        total = forward(F32, turned[0], mine)
        for d in got:
            total = forward(BF16 if d == near - 1 else F32, turned[d], got[d], total)
        return parts_over(total, "par", n_par, True), [mine] + [got[d] for d in range(1, near)]

    op, first = load(operator, start)
    turned = [turn(n_obs, near, d, op) for d in range(near)]
    packed_lanes = shape(scen, LANES, dtype=BF16)
    residual, w, norm, packed = call(
        first_kernel, (image_shape, term_shape, lanes, packed_lanes), (targets, *parts_over(first, "par", n_par, False))
    )
    images, alphas, betas, pieces = [], [], [], []
    gradient = gamma = None
    for index in range(ITERS):
        parts = gradient_parts(w, norm, packed)
        gradient, rounded, alpha = call(
            functools.partial(gradient_kernel, index > 0, near),
            (shape(scen, width), shape(scen, width, dtype=BF16), lanes),
            ((gradient, gamma) if index else tuple(turned)) + tuple(parts),
            None if index else [ANY] * near + [VMEM] * len(parts),
        )
        alphas += [alpha] if index else []
        parts, got = image_parts(rounded)
        pieces += got
        last = index == ITERS - 1
        image, gamma, beta, norm, *more = call(
            functools.partial(image_kernel, index > 0, last),
            (image_shape, lanes, lanes, lanes) + (() if last else (packed_lanes, term_shape)),
            ((image, gamma) if index else ()) + tuple(parts),
        )
        if not last:
            packed, w = more
        images.append(image)
        betas.append(beta)

    norms = norm_parts(norm, n_obs, n_par)
    direction, base = call(
        functools.partial(directions_kernel, n_obs, near, width),
        (shape(scen, columns), shape(scen, columns)),
        (start, *alphas, *betas, *pieces),
    )
    return call(
        functools.partial(last_kernel, len(norms)),
        (shape(scen, columns), image_shape),
        (gamma, direction, base, residual, *norms, *alphas, *images),
    )


def solution(mesh):
    return jax.shard_map(
        functools.partial(shards, mesh.shape["obs"], mesh.shape["par"]),
        mesh=mesh,
        in_specs=(P("obs", "par"), P(None, "obs"), P(None, "par")),
        out_specs=(P(None, "par"), P(None, "obs")),
        check_vma=False,
    )
```

```python
import functools

import jax
import jax.numpy as jnp
from jax import lax
from jax.experimental import pallas as pl
from jax.experimental.pallas import tpu as pltpu
from jax.sharding import PartitionSpec as P

ITERS = 4
EARLY = 4
LIMIT = 8
ADD_FLOPS = 1 << 28
LANES = 128
F32 = jnp.float32
BF16 = jnp.bfloat16
VMEM = pl.BlockSpec(memory_space=pltpu.VMEM)
ANY = pl.BlockSpec(memory_space=pl.ANY)


def shape(*sizes, dtype=F32):
    return jax.ShapeDtypeStruct(sizes, dtype)


def call(body, out, args, specs=None, scratch=(), flops=0, aliases=None, out_specs=None, limit=LIMIT):
    return pl.pallas_call(
        body,
        out_shape=out,
        in_specs=specs if specs is not None else [VMEM] * len(args),
        out_specs=out_specs or jax.tree.map(lambda _: VMEM, out),
        input_output_aliases=aliases or {},
        scratch_shapes=scratch,
        compiler_params=pltpu.CompilerParams(vmem_limit_bytes=limit << 20),
        cost_estimate=pl.CostEstimate(flops=flops, bytes_accessed=1024, transcendentals=0),
    )(*args)


def tree(parts):
    if len(parts) == 1:
        return parts[0]
    half = len(parts) // 2
    return tree(parts[:half]) + tree(parts[half:])


def lane_total(value):
    return jnp.broadcast_to(jnp.sum(value, axis=1, keepdims=True), (value.shape[0], LANES))


def pack_norm(value):
    high = value.astype(BF16).astype(F32)
    rest = value - high
    middle = rest.astype(BF16).astype(F32)
    lane = lax.broadcasted_iota(jnp.int32, value.shape, 1)
    zero = jnp.zeros_like(value)
    return jnp.where(
        lane == 0, high, jnp.where(lane == 1, middle, jnp.where(lane == 2, rest - middle, zero))
    ).astype(BF16)


def unpack_norm(block):
    return lane_total(block.astype(F32))


def split(value, out_ref):
    scen = value.shape[0]
    high = value.astype(BF16)
    out_ref[:scen, :] = high
    out_ref[scen:, :] = (value - high.astype(F32)).astype(BF16)


def bring(chunk, first, last, op_hbm, op_ref, sems):
    copies = []
    for k in range(first, last):
        at = pl.ds(k * chunk, chunk)
        copies.append(pltpu.make_async_copy(op_hbm.at[:, at], op_ref.at[:, at], sems.at[k]))
        copies[-1].start()
    return copies


def early_kernel(chunk, last, op_hbm, op_ref, sems):
    for copy in bring(chunk, 0, last, op_hbm, op_ref, sems):
        copy.wait()


def load_kernel(chunk, first, last, op_hbm, start_ref, early_ref, op_ref, image_ref, sems):
    del early_ref
    copies = bring(chunk, first, last, op_hbm, op_ref, sems)
    total = jnp.zeros(image_ref.shape, F32)
    for k in range(last):
        if k >= first:
            copies[k - first].wait()
        at = pl.ds(k * chunk, chunk)
        total += lax.dot_general(
            start_ref[:, at].astype(BF16), op_ref[:, at], (((1,), (1,)), ((), ())), preferred_element_type=F32
        )
    image_ref[...] = total.astype(BF16)


def load(operator, start):
    rows, columns = operator.shape
    chunk = min(1024, columns)
    pieces = columns // chunk
    first = pieces * EARLY // 16
    whole = shape(rows, columns, dtype=BF16)
    sems = [pltpu.SemaphoreType.DMA((pieces,))]
    early = call(functools.partial(early_kernel, chunk, first), whole, (operator,), [ANY], sems, limit=24)
    return call(
        functools.partial(load_kernel, chunk, first, pieces),
        (whole, shape(start.shape[0], rows, dtype=BF16)),
        (operator, start, early),
        [ANY, VMEM, VMEM],
        sems,
        aliases={2: 0},
        limit=24,
    )


def place(n_obs, near, distance):
    me = lax.axis_index("obs")
    own = me & (near - 1)
    if mirrored(n_obs, near):
        own = own ^ (((me >> 2) & 1) << 1)
    return own ^ distance


def mirrored(n_obs, near):
    return n_obs == 2 * near and near == 4


def backward_kernel(n_obs, near, distance, chunk, op_ref, w_ref, *refs):
    out_ref = refs[-1]
    scen = out_ref.shape[0]
    width = out_ref.shape[1] - LANES * (len(refs) - 1)
    w = w_ref[...]
    base = place(n_obs, near, distance) * width
    for k in range(width // chunk):
        at = pl.ds(pl.multiple_of(base + k * chunk, chunk), chunk)
        both = jnp.dot(w, op_ref[:, at], preferred_element_type=F32)
        out_ref[:, k * chunk : (k + 1) * chunk] = (both[:scen] + both[scen:]).astype(out_ref.dtype)
    for norm_ref in refs[:-1]:
        out_ref[:, width:] = norm_ref[...]


def backward(n_obs, near, distance, op, w, *norm):
    width = op.shape[1] // near
    scen = w.shape[0] // 2
    out = shape(scen, width + LANES, dtype=BF16) if norm else shape(scen, width)
    return call(
        functools.partial(backward_kernel, n_obs, near, distance, min(1024, width)),
        out,
        (op, w, *norm),
    )


def turn_kernel(n_obs, near, distance, op_ref, out_ref):
    width = out_ref.shape[0]
    chunk = min(512, width)
    base = place(n_obs, near, distance) * width
    for first in range(0, width, chunk):
        at = pl.ds(pl.multiple_of(base + first, chunk), chunk)
        out_ref[first : first + chunk, :] = op_ref[:, at].T


def turn(n_obs, near, distance, op):
    rows, columns = op.shape
    return call(
        functools.partial(turn_kernel, n_obs, near, distance), shape(columns // near, rows, dtype=BF16), (op,)
    )


def forward_kernel(turned_ref, v_ref, *refs):
    out_ref = refs[-1]
    width, rows = turned_ref.shape
    v = v_ref[...]
    image = jnp.dot(v, turned_ref[...], preferred_element_type=F32)
    wide = v.astype(F32)
    square = wide * wide
    norm = square[:, :LANES]
    for k in range(1, width // LANES):
        norm += square[:, k * LANES : (k + 1) * LANES]
    norms = [norm]
    for sum_ref in refs[:-1]:
        image += sum_ref[:, :rows]
        norms = [sum_ref[:, at : at + LANES] for at in range(rows, sum_ref.shape[1], LANES)] + norms
    if out_ref.dtype == BF16:
        norms = [pack_norm(lane_total(tree(norms)))]
    out_ref[:, :rows] = image.astype(out_ref.dtype)
    for k, norm in enumerate(norms):
        out_ref[:, rows + k * LANES : rows + (k + 1) * LANES] = norm


def forward(last, turned, v, *total):
    scen, rows = v.shape[0], turned.shape[1]
    if last:
        out = shape(scen, rows + LANES, dtype=BF16)
    else:
        out = shape(scen, (total[0].shape[1] if total else rows) + LANES)
    return call(forward_kernel, out, (turned, v, *total))


def first_kernel(targets_ref, *refs):
    *part_refs, residual_ref, w_ref, norm_ref, packed_ref = refs
    residual = targets_ref[...] - tree([ref[...].astype(F32) for ref in part_refs])
    residual_ref[...] = residual
    norm_ref[...] = jnp.zeros(norm_ref.shape, F32)
    packed_ref[...] = jnp.zeros(packed_ref.shape, BF16)
    split(residual, w_ref)


def image_kernel(later, last, *refs):
    outs = 4 + (not last) * 2
    ins, (image_ref, gamma_ref, beta_ref, norm_ref, *more_refs) = refs[:-outs], refs[-outs:]
    if later:
        old_ref, old_gamma_ref, *ins = ins
    rows = image_ref.shape[1]
    image = tree([ref[:, :rows].astype(F32) for ref in ins])
    gamma = tree([unpack_norm(ref[:, rows:]) for ref in ins])
    beta = jnp.zeros_like(gamma)
    if later:
        beta = gamma / old_gamma_ref[...]
        image += jnp.concatenate([beta] * (rows // LANES), axis=1) * old_ref[...]
    image_ref[...] = image
    gamma_ref[...] = gamma
    beta_ref[...] = beta
    norm = lane_total(image * image)
    norm_ref[...] = norm
    if not last:
        packed_ref, w_ref = more_refs
        packed_ref[...] = pack_norm(norm)
        split(image, w_ref)


def add_kernel(sum_ref, got_ref, out_ref):
    out_ref[...] = sum_ref[...] + got_ref[:, : out_ref.shape[1]].astype(F32)


def near_kernel(order, sum_ref, norm_ref, *refs):
    *got_refs, out_ref = refs
    width = sum_ref.shape[1]
    total = sum_ref[...] + got_refs[-1][:, :width].astype(F32)
    norm = tree([norm_ref[...]] + [unpack_norm(ref[:, width:]) for _, ref in sorted(zip(order, got_refs), key=lambda pair: pair[0])])
    out_ref[:, :width] = total.astype(BF16)
    out_ref[:, width:] = pack_norm(norm)


def far_kernel(normed, *refs):
    *got_refs, out_ref = refs
    width = out_ref.shape[1] - normed * LANES
    out_ref[:, :width] = tree([ref[:, :width].astype(F32) for ref in got_refs]).astype(BF16)
    if normed:
        out_ref[:, width:] = pack_norm(tree([unpack_norm(ref[:, width:]) for ref in got_refs]))


def gradient_kernel(later, before, *refs):
    *ins, gradient_ref, rounded_ref, alpha_ref = refs
    if not later:
        ins = ins[before:]
    if later:
        old_ref, gamma_ref, *ins = ins
    width = gradient_ref.shape[1]
    total = tree([ref[:, :width].astype(F32) for ref in ins])
    if later:
        alpha = gamma_ref[...] / tree([unpack_norm(ref[:, width:]) for ref in ins])
        alpha_ref[...] = alpha
        total = old_ref[...] - jnp.concatenate([alpha] * (width // LANES), axis=1) * total
    else:
        alpha_ref[...] = jnp.zeros(alpha_ref.shape, F32)
    gradient_ref[...] = total
    rounded_ref[...] = total.astype(BF16)


def directions_kernel(n_obs, near, width, start_ref, *refs):
    *ins, direction_ref, solution_ref = refs
    alphas = ins[: ITERS - 1]
    betas = ins[ITERS - 1 : 2 * ITERS - 1]
    pieces = ins[2 * ITERS - 1 :]
    for d in range(near):
        base = place(n_obs, near, d) * width
        for k in range(width // LANES):
            at = pl.ds(pl.multiple_of(base + k * LANES, LANES), LANES)
            here = slice(k * LANES, (k + 1) * LANES)
            solution = start_ref[:, at]
            direction = pieces[d][:, here].astype(F32)
            for index in range(1, ITERS):
                solution += alphas[index - 1][...] * direction
                direction = pieces[index * near + d][:, here].astype(F32) + betas[index][...] * direction
            direction_ref[:, at] = direction
            solution_ref[:, at] = solution


def last_kernel(parts, gamma_ref, direction_ref, base_ref, residual_ref, *refs):
    *ins, out_ref, out_residual_ref = refs
    norms = ins[:parts]
    alphas = ins[parts : parts + ITERS - 1]
    images = ins[parts + ITERS - 1 :]
    alpha = gamma_ref[...] / tree([ref[...] for ref in norms])

    def step(k, _):
        at = pl.ds(pl.multiple_of(k * LANES, LANES), LANES)
        out_ref[:, at] = base_ref[:, at] + alpha * direction_ref[:, at]
        return 0

    lax.fori_loop(0, out_ref.shape[1] // LANES, step, 0, unroll=8)
    residual = residual_ref[...]
    rows = residual.shape[1]
    for index in range(ITERS):
        factor = alpha if index == ITERS - 1 else alphas[index][...]
        residual -= jnp.concatenate([factor] * (rows // LANES), axis=1) * images[index][...]
    out_residual_ref[...] = residual


def exchange(value, axis, size, distance):
    return lax.ppermute(value, axis, [(i, i ^ distance) for i in range(size)])


def stages(size, stride=1):
    found = []
    while stride < size:
        members = 4 if size // stride % 4 == 0 else 2
        found.append((stride, members))
        stride *= members
    return found


def exchanged(value, axis, size, stride, members):
    return [value] + [exchange(value, axis, size, k * stride) for k in range(1, members)]


def parts_over(value, axis, size, normed):
    parts = [value]
    for index, (stride, members) in enumerate(stages(size)):
        if index:
            value = call(functools.partial(far_kernel, normed), jax.ShapeDtypeStruct(value.shape, BF16), parts)
        parts = exchanged(value, axis, size, stride, members)
    return parts


def norm_kernel(mine_ref, *refs):
    first_ref, *got_refs, out_ref = refs
    own = jnp.where((lax.axis_index("par") & 1) == 0, mine_ref[...], first_ref[...])
    out_ref[...] = tree([own] + [ref[...] for ref in got_refs])


def norm_parts(norm, n_obs, n_par):
    half = n_obs // 2
    got = []
    for k in range(half):
        pairs = []
        for at in range(n_obs):
            for member in range(n_par):
                there = at ^ (half + k if member % 2 or not k else k)
                pairs.append((at * n_par + member, there * n_par + member))
        got.append(lax.ppermute(norm, ("obs", "par"), pairs))
    return exchanged(call(norm_kernel, jax.ShapeDtypeStruct(norm.shape, F32), (norm, *got)), "par", n_par, 1, 2)


def shards(n_obs, n_par, operator, targets, start):
    rows, columns = operator.shape
    scen = start.shape[0]
    near = 4 if n_obs % 4 == 0 else n_obs
    width = columns // near
    lanes = shape(scen, LANES)
    image_shape = shape(scen, rows)
    term_shape = shape(2 * scen, rows, dtype=BF16)

    def gradient_parts(w, norm, packed):
        order = (2, 1, 3) if near == 4 else tuple(range(1, near))
        got = {d: exchange(backward(n_obs, near, d, op, w, packed), "obs", n_obs, d) for d in order}
        total = backward(n_obs, near, 0, op, w)
        for d in order[:-1]:
            total = call(add_kernel, shape(scen, width), (total, got[d]), flops=ADD_FLOPS)
        both = shape(scen, width + LANES, dtype=BF16)
        value = call(functools.partial(near_kernel, order), both, (total, norm, *(got[d] for d in order)))
        parts = [value]
        for index, (stride, members) in enumerate(stages(n_obs, near)):
            if index:
                value = call(functools.partial(far_kernel, True), both, parts)
            if mirrored(n_obs, near):
                stride += 2
            parts = exchanged(value, "obs", n_obs, stride, members)
        return parts

    def image_parts(mine):
        got = {d: exchange(mine, "obs", n_obs, d) for d in range(1, near)}
        total = forward(near == 1, turned[0], mine)
        for d in got:
            total = forward(d == near - 1, turned[d], got[d], total)
        return parts_over(total, "par", n_par, True), [mine] + [got[d] for d in range(1, near)]

    op, first = load(operator, start)
    turned = [turn(n_obs, near, d, op) for d in range(near)]
    packed_lanes = shape(scen, LANES, dtype=BF16)
    residual, w, norm, packed = call(
        first_kernel, (image_shape, term_shape, lanes, packed_lanes), (targets, *parts_over(first, "par", n_par, False))
    )
    images, alphas, betas, pieces = [], [], [], []
    gradient = gamma = None
    for index in range(ITERS):
        parts = gradient_parts(w, norm, packed)
        gradient, rounded, alpha = call(
            functools.partial(gradient_kernel, index > 0, near),
            (shape(scen, width), shape(scen, width, dtype=BF16), lanes),
            ((gradient, gamma) if index else tuple(turned)) + tuple(parts),
            None if index else [ANY] * near + [VMEM] * len(parts),
        )
        alphas += [alpha] if index else []
        parts, got = image_parts(rounded)
        pieces += got
        last = index == ITERS - 1
        image, gamma, beta, norm, *more = call(
            functools.partial(image_kernel, index > 0, last),
            (image_shape, lanes, lanes, lanes) + (() if last else (packed_lanes, term_shape)),
            ((image, gamma) if index else ()) + tuple(parts),
        )
        if not last:
            packed, w = more
        images.append(image)
        betas.append(beta)

    norms = norm_parts(norm, n_obs, n_par)
    direction, base = call(
        functools.partial(directions_kernel, n_obs, near, width),
        (shape(scen, columns), shape(scen, columns)),
        (start, *alphas, *betas, *pieces),
    )
    return call(
        functools.partial(last_kernel, len(norms)),
        (shape(scen, columns), image_shape),
        (gamma, direction, base, residual, *norms, *alphas, *images),
    )


def solution(mesh):
    return jax.shard_map(
        functools.partial(shards, mesh.shape["obs"], mesh.shape["par"]),
        mesh=mesh,
        in_specs=(P("obs", "par"), P(None, "obs"), P(None, "par")),
        out_specs=(P(None, "par"), P(None, "obs")),
        check_vma=False,
    )
```

```python
import functools

import jax
import jax.numpy as jnp
from jax import lax
from jax.experimental import pallas as pl
from jax.experimental.pallas import tpu as pltpu
from jax.sharding import PartitionSpec as P

ITERS = 4
EARLY = 4
RS_ORDERS = ((2, 1, 3), (2, 1, 3))
AG_ORDERS = ((3, 2, 1), (1, 2, 3))
LIMIT = 8
ADD_FLOPS = 1 << 28
LANES = 128
F32 = jnp.float32
BF16 = jnp.bfloat16
VMEM = pl.BlockSpec(memory_space=pltpu.VMEM)
ANY = pl.BlockSpec(memory_space=pl.ANY)


def shape(*sizes, dtype=F32):
    return jax.ShapeDtypeStruct(sizes, dtype)


def call(body, out, args, specs=None, scratch=(), flops=0, aliases=None, out_specs=None, limit=LIMIT):
    return pl.pallas_call(
        body,
        out_shape=out,
        in_specs=specs if specs is not None else [VMEM] * len(args),
        out_specs=out_specs or jax.tree.map(lambda _: VMEM, out),
        input_output_aliases=aliases or {},
        scratch_shapes=scratch,
        compiler_params=pltpu.CompilerParams(vmem_limit_bytes=limit << 20),
        cost_estimate=pl.CostEstimate(flops=flops, bytes_accessed=1024, transcendentals=0),
    )(*args)


def tree(parts):
    if len(parts) == 1:
        return parts[0]
    half = len(parts) // 2
    return tree(parts[:half]) + tree(parts[half:])


def lane_total(value):
    return jnp.broadcast_to(jnp.sum(value, axis=1, keepdims=True), (value.shape[0], LANES))


def pack_norm(value):
    high = value.astype(BF16).astype(F32)
    rest = value - high
    middle = rest.astype(BF16).astype(F32)
    lane = lax.broadcasted_iota(jnp.int32, value.shape, 1)
    zero = jnp.zeros_like(value)
    return jnp.where(
        lane == 0, high, jnp.where(lane == 1, middle, jnp.where(lane == 2, rest - middle, zero))
    ).astype(BF16)


def unpack_norm(block):
    return lane_total(block.astype(F32))


def split(value, out_ref):
    scen = value.shape[0]
    high = value.astype(BF16)
    out_ref[:scen, :] = high
    out_ref[scen:, :] = (value - high.astype(F32)).astype(BF16)


def bring(chunk, first, last, op_hbm, op_ref, sems):
    copies = []
    for k in range(first, last):
        at = pl.ds(k * chunk, chunk)
        copies.append(pltpu.make_async_copy(op_hbm.at[:, at], op_ref.at[:, at], sems.at[k]))
        copies[-1].start()
    return copies


def early_kernel(chunk, last, op_hbm, op_ref, sems):
    for copy in bring(chunk, 0, last, op_hbm, op_ref, sems):
        copy.wait()


def load_kernel(chunk, first, last, op_hbm, start_ref, early_ref, op_ref, image_ref, sems):
    del early_ref
    copies = bring(chunk, first, last, op_hbm, op_ref, sems)
    total = jnp.zeros(image_ref.shape, F32)
    for k in range(last):
        if k >= first:
            copies[k - first].wait()
        at = pl.ds(k * chunk, chunk)
        total += lax.dot_general(
            start_ref[:, at].astype(BF16), op_ref[:, at], (((1,), (1,)), ((), ())), preferred_element_type=F32
        )
    image_ref[...] = total.astype(BF16)


def load(operator, start):
    rows, columns = operator.shape
    chunk = min(1024, columns)
    pieces = columns // chunk
    first = pieces * EARLY // 16
    whole = shape(rows, columns, dtype=BF16)
    sems = [pltpu.SemaphoreType.DMA((pieces,))]
    early = call(functools.partial(early_kernel, chunk, first), whole, (operator,), [ANY], sems, limit=24)
    return call(
        functools.partial(load_kernel, chunk, first, pieces),
        (whole, shape(start.shape[0], rows, dtype=BF16)),
        (operator, start, early),
        [ANY, VMEM, VMEM],
        sems,
        aliases={2: 0},
        limit=24,
    )


def odd():
    return (lax.axis_index("par") & 1) == 1


def place(n_obs, near, distances):
    me = lax.axis_index("obs")
    own = me & (near - 1)
    if mirrored(n_obs, near):
        own = own ^ (((me >> 2) & 1) << 1)
    even_one, odd_one = distances
    return own ^ (even_one if even_one == odd_one else jnp.where(odd(), odd_one, even_one))


def slots(near, orders):
    return list(zip(*orders)) if near == 4 else [(d, d) for d in range(1, near)]


def mirrored(n_obs, near):
    return n_obs == 2 * near and near == 4


def backward_kernel(n_obs, near, distance, chunk, op_ref, w_ref, *refs):
    out_ref = refs[-1]
    scen = out_ref.shape[0]
    width = out_ref.shape[1] - LANES * (len(refs) - 1)
    w = w_ref[...]
    base = place(n_obs, near, distance) * width
    for k in range(width // chunk):
        at = pl.ds(pl.multiple_of(base + k * chunk, chunk), chunk)
        both = jnp.dot(w, op_ref[:, at], preferred_element_type=F32)
        out_ref[:, k * chunk : (k + 1) * chunk] = (both[:scen] + both[scen:]).astype(out_ref.dtype)
    for norm_ref in refs[:-1]:
        out_ref[:, width:] = norm_ref[...]


def backward(n_obs, near, distance, op, w, *norm):
    width = op.shape[1] // near
    scen = w.shape[0] // 2
    out = shape(scen, width + LANES, dtype=BF16) if norm else shape(scen, width)
    return call(
        functools.partial(backward_kernel, n_obs, near, distance, min(1024, width)),
        out,
        (op, w, *norm),
    )


def turn_kernel(n_obs, near, distance, op_ref, out_ref):
    width = out_ref.shape[0]
    chunk = min(512, width)
    base = place(n_obs, near, distance) * width
    for first in range(0, width, chunk):
        at = pl.ds(pl.multiple_of(base + first, chunk), chunk)
        out_ref[first : first + chunk, :] = op_ref[:, at].T


def turn(n_obs, near, distance, op):
    rows, columns = op.shape
    return call(
        functools.partial(turn_kernel, n_obs, near, distance), shape(columns // near, rows, dtype=BF16), (op,)
    )


def forward_kernel(turned_ref, v_ref, *refs):
    out_ref = refs[-1]
    width, rows = turned_ref.shape
    v = v_ref[...]
    image = jnp.dot(v, turned_ref[...], preferred_element_type=F32)
    wide = v.astype(F32)
    square = wide * wide
    norm = square[:, :LANES]
    for k in range(1, width // LANES):
        norm += square[:, k * LANES : (k + 1) * LANES]
    norms = [norm]
    for sum_ref in refs[:-1]:
        image += sum_ref[:, :rows]
        norms = [sum_ref[:, at : at + LANES] for at in range(rows, sum_ref.shape[1], LANES)] + norms
    if out_ref.dtype == BF16:
        norms = [pack_norm(lane_total(tree(norms)))]
    out_ref[:, :rows] = image.astype(out_ref.dtype)
    for k, norm in enumerate(norms):
        out_ref[:, rows + k * LANES : rows + (k + 1) * LANES] = norm


def forward(last, turned, v, *total):
    scen, rows = v.shape[0], turned.shape[1]
    if last:
        out = shape(scen, rows + LANES, dtype=BF16)
    else:
        out = shape(scen, (total[0].shape[1] if total else rows) + LANES)
    return call(forward_kernel, out, (turned, v, *total))


def first_kernel(targets_ref, *refs):
    *part_refs, residual_ref, w_ref, norm_ref, packed_ref = refs
    residual = targets_ref[...] - tree([ref[...].astype(F32) for ref in part_refs])
    residual_ref[...] = residual
    norm_ref[...] = jnp.zeros(norm_ref.shape, F32)
    packed_ref[...] = jnp.zeros(packed_ref.shape, BF16)
    split(residual, w_ref)


def image_kernel(later, last, *refs):
    outs = 4 + (not last) * 2
    ins, (image_ref, gamma_ref, beta_ref, norm_ref, *more_refs) = refs[:-outs], refs[-outs:]
    if later:
        old_ref, old_gamma_ref, *ins = ins
    rows = image_ref.shape[1]
    image = tree([ref[:, :rows].astype(F32) for ref in ins])
    gamma = tree([unpack_norm(ref[:, rows:]) for ref in ins])
    beta = jnp.zeros_like(gamma)
    if later:
        beta = gamma / old_gamma_ref[...]
        image += jnp.concatenate([beta] * (rows // LANES), axis=1) * old_ref[...]
    image_ref[...] = image
    gamma_ref[...] = gamma
    beta_ref[...] = beta
    norm = lane_total(image * image)
    norm_ref[...] = norm
    if not last:
        packed_ref, w_ref = more_refs
        packed_ref[...] = pack_norm(norm)
        split(image, w_ref)


def add_kernel(sum_ref, got_ref, out_ref):
    out_ref[...] = sum_ref[...] + got_ref[:, : out_ref.shape[1]].astype(F32)


def by_distance(order, member):
    return sorted(range(len(order)), key=lambda k: order[k][member])


def near_kernel(order, sum_ref, norm_ref, *refs):
    *got_refs, out_ref = refs
    width = sum_ref.shape[1]
    total = sum_ref[...] + got_refs[-1][:, :width].astype(F32)
    norms = [unpack_norm(ref[:, width:]) for ref in got_refs]
    even, other = ([norm_ref[...]] + [norms[k] for k in by_distance(order, member)] for member in range(2))
    norm = jnp.where(odd(), tree(other), tree(even))
    out_ref[:, :width] = total.astype(BF16)
    out_ref[:, width:] = pack_norm(norm)


def far_kernel(normed, *refs):
    *got_refs, out_ref = refs
    width = out_ref.shape[1] - normed * LANES
    out_ref[:, :width] = tree([ref[:, :width].astype(F32) for ref in got_refs]).astype(BF16)
    if normed:
        out_ref[:, width:] = pack_norm(tree([unpack_norm(ref[:, width:]) for ref in got_refs]))


def gradient_kernel(later, before, *refs):
    *ins, gradient_ref, rounded_ref, alpha_ref = refs
    if not later:
        ins = ins[before:]
    if later:
        old_ref, gamma_ref, *ins = ins
    width = gradient_ref.shape[1]
    total = tree([ref[:, :width].astype(F32) for ref in ins])
    if later:
        alpha = gamma_ref[...] / tree([unpack_norm(ref[:, width:]) for ref in ins])
        alpha_ref[...] = alpha
        total = old_ref[...] - jnp.concatenate([alpha] * (width // LANES), axis=1) * total
    else:
        alpha_ref[...] = jnp.zeros(alpha_ref.shape, F32)
    gradient_ref[...] = total
    rounded_ref[...] = total.astype(BF16)


def directions_kernel(n_obs, near, width, start_ref, *refs):
    *ins, direction_ref, solution_ref = refs
    alphas = ins[: ITERS - 1]
    betas = ins[ITERS - 1 : 2 * ITERS - 1]
    pieces = ins[2 * ITERS - 1 :]
    for d, distances in enumerate([(0, 0)] + slots(near, AG_ORDERS)):
        base = place(n_obs, near, distances) * width
        for k in range(width // LANES):
            at = pl.ds(pl.multiple_of(base + k * LANES, LANES), LANES)
            here = slice(k * LANES, (k + 1) * LANES)
            solution = start_ref[:, at]
            direction = pieces[d][:, here].astype(F32)
            for index in range(1, ITERS):
                solution += alphas[index - 1][...] * direction
                direction = pieces[index * near + d][:, here].astype(F32) + betas[index][...] * direction
            direction_ref[:, at] = direction
            solution_ref[:, at] = solution


def last_kernel(parts, gamma_ref, direction_ref, base_ref, residual_ref, *refs):
    *ins, out_ref, out_residual_ref = refs
    norms = ins[:parts]
    alphas = ins[parts : parts + ITERS - 1]
    images = ins[parts + ITERS - 1 :]
    alpha = gamma_ref[...] / tree([ref[...] for ref in norms])

    def step(k, _):
        at = pl.ds(pl.multiple_of(k * LANES, LANES), LANES)
        out_ref[:, at] = base_ref[:, at] + alpha * direction_ref[:, at]
        return 0

    lax.fori_loop(0, out_ref.shape[1] // LANES, step, 0, unroll=8)
    residual = residual_ref[...]
    rows = residual.shape[1]
    for index in range(ITERS):
        factor = alpha if index == ITERS - 1 else alphas[index][...]
        residual -= jnp.concatenate([factor] * (rows // LANES), axis=1) * images[index][...]
    out_residual_ref[...] = residual


def exchange(value, axis, size, distance):
    return lax.ppermute(value, axis, [(i, i ^ distance) for i in range(size)])


def exchange_slot(value, n_obs, n_par, distances):
    pairs = []
    for at in range(n_obs):
        for member in range(n_par):
            pairs.append((at * n_par + member, (at ^ distances[member % 2]) * n_par + member))
    return lax.ppermute(value, ("obs", "par"), pairs)


def stages(size, stride=1):
    found = []
    while stride < size:
        members = 4 if size // stride % 4 == 0 else 2
        found.append((stride, members))
        stride *= members
    return found


def exchanged(value, axis, size, stride, members):
    return [value] + [exchange(value, axis, size, k * stride) for k in range(1, members)]


def parts_over(value, axis, size, normed):
    parts = [value]
    for index, (stride, members) in enumerate(stages(size)):
        if index:
            value = call(functools.partial(far_kernel, normed), jax.ShapeDtypeStruct(value.shape, BF16), parts)
        parts = exchanged(value, axis, size, stride, members)
    return parts


def norm_kernel(mine_ref, *refs):
    first_ref, *got_refs, out_ref = refs
    own = jnp.where((lax.axis_index("par") & 1) == 0, mine_ref[...], first_ref[...])
    out_ref[...] = tree([own] + [ref[...] for ref in got_refs])


def norm_parts(norm, n_obs, n_par):
    half = n_obs // 2
    got = []
    for k in range(half):
        pairs = []
        for at in range(n_obs):
            for member in range(n_par):
                there = at ^ (half + k if member % 2 or not k else k)
                pairs.append((at * n_par + member, there * n_par + member))
        got.append(lax.ppermute(norm, ("obs", "par"), pairs))
    return exchanged(call(norm_kernel, jax.ShapeDtypeStruct(norm.shape, F32), (norm, *got)), "par", n_par, 1, 2)


def shards(n_obs, n_par, operator, targets, start):
    rows, columns = operator.shape
    scen = start.shape[0]
    near = 4 if n_obs % 4 == 0 else n_obs
    width = columns // near
    lanes = shape(scen, LANES)
    image_shape = shape(scen, rows)
    term_shape = shape(2 * scen, rows, dtype=BF16)

    def gradient_parts(w, norm, packed):
        order = slots(near, RS_ORDERS)
        got = [exchange_slot(backward(n_obs, near, d, op, w, packed), n_obs, n_par, d) for d in order]
        total = backward(n_obs, near, (0, 0), op, w)
        for piece in got[:-1]:
            total = call(add_kernel, shape(scen, width), (total, piece), flops=ADD_FLOPS)
        both = shape(scen, width + LANES, dtype=BF16)
        value = call(functools.partial(near_kernel, order), both, (total, norm, *got))
        parts = [value]
        for index, (stride, members) in enumerate(stages(n_obs, near)):
            if index:
                value = call(functools.partial(far_kernel, True), both, parts)
            if mirrored(n_obs, near):
                stride += 2
            parts = exchanged(value, "obs", n_obs, stride, members)
        return parts

    def image_parts(mine):
        got = [exchange_slot(mine, n_obs, n_par, d) for d in slots(near, AG_ORDERS)]
        total = forward(near == 1, turned[0], mine)
        for k, piece in enumerate(got):
            total = forward(k == len(got) - 1, turned[k + 1], piece, total)
        return parts_over(total, "par", n_par, True), [mine] + got

    op, first = load(operator, start)
    turned = [turn(n_obs, near, d, op) for d in [(0, 0)] + slots(near, AG_ORDERS)]
    packed_lanes = shape(scen, LANES, dtype=BF16)
    residual, w, norm, packed = call(
        first_kernel, (image_shape, term_shape, lanes, packed_lanes), (targets, *parts_over(first, "par", n_par, False))
    )
    images, alphas, betas, pieces = [], [], [], []
    gradient = gamma = None
    for index in range(ITERS):
        parts = gradient_parts(w, norm, packed)
        gradient, rounded, alpha = call(
            functools.partial(gradient_kernel, index > 0, near),
            (shape(scen, width), shape(scen, width, dtype=BF16), lanes),
            ((gradient, gamma) if index else tuple(turned)) + tuple(parts),
            None if index else [ANY] * near + [VMEM] * len(parts),
        )
        alphas += [alpha] if index else []
        parts, got = image_parts(rounded)
        pieces += got
        last = index == ITERS - 1
        image, gamma, beta, norm, *more = call(
            functools.partial(image_kernel, index > 0, last),
            (image_shape, lanes, lanes, lanes) + (() if last else (packed_lanes, term_shape)),
            ((image, gamma) if index else ()) + tuple(parts),
        )
        if not last:
            packed, w = more
        images.append(image)
        betas.append(beta)

    norms = norm_parts(norm, n_obs, n_par)
    direction, base = call(
        functools.partial(directions_kernel, n_obs, near, width),
        (shape(scen, columns), shape(scen, columns)),
        (start, *alphas, *betas, *pieces),
    )
    return call(
        functools.partial(last_kernel, len(norms)),
        (shape(scen, columns), image_shape),
        (gamma, direction, base, residual, *norms, *alphas, *images),
    )


def solution(mesh):
    return jax.shard_map(
        functools.partial(shards, mesh.shape["obs"], mesh.shape["par"]),
        mesh=mesh,
        in_specs=(P("obs", "par"), P(None, "obs"), P(None, "par")),
        out_specs=(P(None, "par"), P(None, "obs")),
        check_vma=False,
    )
```

```python
import functools

import jax
import jax.numpy as jnp
from jax import lax
from jax.experimental import pallas as pl
from jax.experimental.pallas import tpu as pltpu
from jax.sharding import PartitionSpec as P

ITERS = 4
EARLY = 4
RS_ORDERS = ((2, 1, 3), (2, 1, 3))
AG_ORDERS = ((3, 2, 1), (1, 2, 3))
LIMIT = 8
ADD_FLOPS = 1 << 28
LANES = 128
F32 = jnp.float32
BF16 = jnp.bfloat16
VMEM = pl.BlockSpec(memory_space=pltpu.VMEM)
ANY = pl.BlockSpec(memory_space=pl.ANY)


def shape(*sizes, dtype=F32):
    return jax.ShapeDtypeStruct(sizes, dtype)


def call(body, out, args, specs=None, scratch=(), flops=0, aliases=None, out_specs=None, limit=LIMIT):
    return pl.pallas_call(
        body,
        out_shape=out,
        in_specs=specs if specs is not None else [VMEM] * len(args),
        out_specs=out_specs or jax.tree.map(lambda _: VMEM, out),
        input_output_aliases=aliases or {},
        scratch_shapes=scratch,
        compiler_params=pltpu.CompilerParams(vmem_limit_bytes=limit << 20),
        cost_estimate=pl.CostEstimate(flops=flops, bytes_accessed=1024, transcendentals=0),
    )(*args)


def tree(parts):
    if len(parts) == 1:
        return parts[0]
    half = len(parts) // 2
    return tree(parts[:half]) + tree(parts[half:])


def lane_total(value):
    return jnp.broadcast_to(jnp.sum(value, axis=1, keepdims=True), (value.shape[0], LANES))


def pack_norm(value):
    high = value.astype(BF16).astype(F32)
    rest = value - high
    middle = rest.astype(BF16).astype(F32)
    lane = lax.broadcasted_iota(jnp.int32, value.shape, 1)
    zero = jnp.zeros_like(value)
    return jnp.where(
        lane == 0, high, jnp.where(lane == 1, middle, jnp.where(lane == 2, rest - middle, zero))
    ).astype(BF16)


def unpack_norm(block):
    return lane_total(block.astype(F32))


def split(value, out_ref):
    scen = value.shape[0]
    high = value.astype(BF16)
    out_ref[:scen, :] = high
    out_ref[scen:, :] = (value - high.astype(F32)).astype(BF16)


def bring(chunk, first, last, op_hbm, op_ref, sems):
    copies = []
    for k in range(first, last):
        at = pl.ds(k * chunk, chunk)
        copies.append(pltpu.make_async_copy(op_hbm.at[:, at], op_ref.at[:, at], sems.at[k]))
        copies[-1].start()
    return copies


def early_kernel(chunk, last, op_hbm, op_ref, sems):
    for copy in bring(chunk, 0, last, op_hbm, op_ref, sems):
        copy.wait()


def load_kernel(chunk, first, last, op_hbm, start_ref, early_ref, op_ref, image_ref, sems):
    del early_ref
    copies = bring(chunk, first, last, op_hbm, op_ref, sems)
    total = jnp.zeros(image_ref.shape, F32)
    for k in range(last):
        if k >= first:
            copies[k - first].wait()
        at = pl.ds(k * chunk, chunk)
        total += lax.dot_general(
            start_ref[:, at].astype(BF16), op_ref[:, at], (((1,), (1,)), ((), ())), preferred_element_type=F32
        )
    image_ref[...] = total.astype(BF16)


def load(operator, start):
    rows, columns = operator.shape
    chunk = min(1024, columns)
    pieces = columns // chunk
    first = pieces * EARLY // 16
    whole = shape(rows, columns, dtype=BF16)
    sems = [pltpu.SemaphoreType.DMA((pieces,))]
    early = call(functools.partial(early_kernel, chunk, first), whole, (operator,), [ANY], sems, limit=24)
    return call(
        functools.partial(load_kernel, chunk, first, pieces),
        (whole, shape(start.shape[0], rows, dtype=BF16)),
        (operator, start, early),
        [ANY, VMEM, VMEM],
        sems,
        aliases={2: 0},
        limit=24,
    )


def odd():
    return (lax.axis_index("par") & 1) == 1


def place(n_obs, near, distances):
    me = lax.axis_index("obs")
    own = me & (near - 1)
    if mirrored(n_obs, near):
        own = own ^ (((me >> 2) & 1) << 1)
    even_one, odd_one = distances
    return own ^ (even_one if even_one == odd_one else jnp.where(odd(), odd_one, even_one))


def slots(near, orders):
    return list(zip(*orders)) if near == 4 else [(d, d) for d in range(1, near)]


def mirrored(n_obs, near):
    return n_obs == 2 * near and near == 4


def backward_kernel(n_obs, near, distance, chunk, op_ref, w_ref, *refs):
    out_ref = refs[-1]
    scen = out_ref.shape[0]
    width = out_ref.shape[1] - LANES * (len(refs) - 1)
    w = w_ref[...]
    base = place(n_obs, near, distance) * width
    for k in range(width // chunk):
        at = pl.ds(pl.multiple_of(base + k * chunk, chunk), chunk)
        both = jnp.dot(w, op_ref[:, at], preferred_element_type=F32)
        out_ref[:, k * chunk : (k + 1) * chunk] = (both[:scen] + both[scen:]).astype(out_ref.dtype)
    for norm_ref in refs[:-1]:
        out_ref[:, width:] = norm_ref[...]


def backward(n_obs, near, distance, op, w, *norm):
    width = op.shape[1] // near
    scen = w.shape[0] // 2
    out = shape(scen, width + LANES, dtype=BF16) if norm else shape(scen, width)
    return call(
        functools.partial(backward_kernel, n_obs, near, distance, min(1024, width)),
        out,
        (op, w, *norm),
    )


def turn_kernel(n_obs, near, distance, op_ref, out_ref):
    width = out_ref.shape[0]
    chunk = min(512, width)
    base = place(n_obs, near, distance) * width
    for first in range(0, width, chunk):
        at = pl.ds(pl.multiple_of(base + first, chunk), chunk)
        out_ref[first : first + chunk, :] = op_ref[:, at].T


def turn(n_obs, near, distance, op):
    rows, columns = op.shape
    return call(
        functools.partial(turn_kernel, n_obs, near, distance), shape(columns // near, rows, dtype=BF16), (op,)
    )


def forward_kernel(turned_ref, v_ref, *refs):
    out_ref = refs[-1]
    width, rows = turned_ref.shape
    v = v_ref[...]
    image = jnp.dot(v, turned_ref[...], preferred_element_type=F32)
    wide = v.astype(F32)
    square = wide * wide
    norm = square[:, :LANES]
    for k in range(1, width // LANES):
        norm += square[:, k * LANES : (k + 1) * LANES]
    norms = [norm]
    for sum_ref in refs[:-1]:
        image += sum_ref[:, :rows]
        norms = [sum_ref[:, at : at + LANES] for at in range(rows, sum_ref.shape[1], LANES)] + norms
    if out_ref.dtype == BF16:
        norms = [pack_norm(lane_total(tree(norms)))]
    out_ref[:, :rows] = image.astype(out_ref.dtype)
    for k, norm in enumerate(norms):
        out_ref[:, rows + k * LANES : rows + (k + 1) * LANES] = norm


def forward(last, turned, v, *total):
    scen, rows = v.shape[0], turned.shape[1]
    if last:
        out = shape(scen, rows + LANES, dtype=BF16)
    else:
        out = shape(scen, (total[0].shape[1] if total else rows) + LANES)
    return call(forward_kernel, out, (turned, v, *total))


def first_kernel(targets_ref, *refs):
    *part_refs, residual_ref, w_ref, norm_ref, packed_ref = refs
    residual = targets_ref[...] - tree([ref[...].astype(F32) for ref in part_refs])
    residual_ref[...] = residual
    norm_ref[...] = jnp.zeros(norm_ref.shape, F32)
    packed_ref[...] = jnp.zeros(packed_ref.shape, BF16)
    split(residual, w_ref)


def image_kernel(later, last, *refs):
    outs = 4 + (not last) * 2
    ins, (image_ref, gamma_ref, beta_ref, norm_ref, *more_refs) = refs[:-outs], refs[-outs:]
    if later:
        old_ref, old_gamma_ref, *ins = ins
    rows = image_ref.shape[1]
    image = tree([ref[:, :rows].astype(F32) for ref in ins])
    gamma = tree([unpack_norm(ref[:, rows:]) for ref in ins])
    beta = jnp.zeros_like(gamma)
    if later:
        beta = gamma / old_gamma_ref[...]
        image += jnp.concatenate([beta] * (rows // LANES), axis=1) * old_ref[...]
    image_ref[...] = image
    gamma_ref[...] = gamma
    beta_ref[...] = beta
    norm = lane_total(image * image)
    norm_ref[...] = norm
    if not last:
        packed_ref, w_ref = more_refs
        packed_ref[...] = pack_norm(norm)
        split(image, w_ref)


def add_kernel(sum_ref, got_ref, out_ref):
    out_ref[...] = sum_ref[...] + got_ref[:, : out_ref.shape[1]].astype(F32)


def by_distance(order, member):
    return sorted(range(len(order)), key=lambda k: order[k][member])


def near_kernel(order, before, sum_ref, norm_ref, *refs):
    *got_refs, out_ref = refs[before:]
    width = sum_ref.shape[1]
    total = sum_ref[...] + got_refs[-1][:, :width].astype(F32)
    norms = [unpack_norm(ref[:, width:]) for ref in got_refs]
    even, other = ([norm_ref[...]] + [norms[k] for k in by_distance(order, member)] for member in range(2))
    norm = jnp.where(odd(), tree(other), tree(even))
    out_ref[:, :width] = total.astype(BF16)
    out_ref[:, width:] = pack_norm(norm)


def far_kernel(normed, *refs):
    *got_refs, out_ref = refs
    width = out_ref.shape[1] - normed * LANES
    out_ref[:, :width] = tree([ref[:, :width].astype(F32) for ref in got_refs]).astype(BF16)
    if normed:
        out_ref[:, width:] = pack_norm(tree([unpack_norm(ref[:, width:]) for ref in got_refs]))


def gradient_kernel(later, before, *refs):
    *ins, gradient_ref, rounded_ref, alpha_ref = refs
    if not later:
        ins = ins[before:]
    if later:
        old_ref, gamma_ref, *ins = ins
    width = gradient_ref.shape[1]
    total = tree([ref[:, :width].astype(F32) for ref in ins])
    if later:
        alpha = gamma_ref[...] / tree([unpack_norm(ref[:, width:]) for ref in ins])
        alpha_ref[...] = alpha
        total = old_ref[...] - jnp.concatenate([alpha] * (width // LANES), axis=1) * total
    else:
        alpha_ref[...] = jnp.zeros(alpha_ref.shape, F32)
    gradient_ref[...] = total
    rounded_ref[...] = total.astype(BF16)


def directions_kernel(n_obs, near, width, start_ref, *refs):
    *ins, direction_ref, solution_ref = refs
    alphas = ins[: ITERS - 1]
    betas = ins[ITERS - 1 : 2 * ITERS - 1]
    pieces = ins[2 * ITERS - 1 :]
    for d, distances in enumerate([(0, 0)] + slots(near, AG_ORDERS)):
        base = place(n_obs, near, distances) * width
        for k in range(width // LANES):
            at = pl.ds(pl.multiple_of(base + k * LANES, LANES), LANES)
            here = slice(k * LANES, (k + 1) * LANES)
            solution = start_ref[:, at]
            direction = pieces[d][:, here].astype(F32)
            for index in range(1, ITERS):
                solution += alphas[index - 1][...] * direction
                direction = pieces[index * near + d][:, here].astype(F32) + betas[index][...] * direction
            direction_ref[:, at] = direction
            solution_ref[:, at] = solution


def last_kernel(parts, gamma_ref, direction_ref, base_ref, residual_ref, *refs):
    *ins, out_ref, out_residual_ref = refs
    norms = ins[:parts]
    alphas = ins[parts : parts + ITERS - 1]
    images = ins[parts + ITERS - 1 :]
    alpha = gamma_ref[...] / tree([ref[...] for ref in norms])

    def step(k, _):
        at = pl.ds(pl.multiple_of(k * LANES, LANES), LANES)
        out_ref[:, at] = base_ref[:, at] + alpha * direction_ref[:, at]
        return 0

    lax.fori_loop(0, out_ref.shape[1] // LANES, step, 0, unroll=8)
    residual = residual_ref[...]
    rows = residual.shape[1]
    for index in range(ITERS):
        factor = alpha if index == ITERS - 1 else alphas[index][...]
        residual -= jnp.concatenate([factor] * (rows // LANES), axis=1) * images[index][...]
    out_residual_ref[...] = residual


def exchange(value, axis, size, distance):
    return lax.ppermute(value, axis, [(i, i ^ distance) for i in range(size)])


def exchange_slot(value, n_obs, n_par, distances):
    pairs = []
    for at in range(n_obs):
        for member in range(n_par):
            pairs.append((at * n_par + member, (at ^ distances[member % 2]) * n_par + member))
    return lax.ppermute(value, ("obs", "par"), pairs)


def stages(size, stride=1):
    found = []
    while stride < size:
        members = 4 if size // stride % 4 == 0 else 2
        found.append((stride, members))
        stride *= members
    return found


def exchanged(value, axis, size, stride, members):
    return [value] + [exchange(value, axis, size, k * stride) for k in range(1, members)]


def parts_over(value, axis, size, normed):
    parts = [value]
    for index, (stride, members) in enumerate(stages(size)):
        if index:
            value = call(functools.partial(far_kernel, normed), jax.ShapeDtypeStruct(value.shape, BF16), parts)
        parts = exchanged(value, axis, size, stride, members)
    return parts


def norm_kernel(mine_ref, *refs):
    first_ref, *got_refs, out_ref = refs
    own = jnp.where((lax.axis_index("par") & 1) == 0, mine_ref[...], first_ref[...])
    out_ref[...] = tree([own] + [ref[...] for ref in got_refs])


def norm_parts(norm, n_obs, n_par):
    half = n_obs // 2
    got = []
    for k in range(half):
        pairs = []
        for at in range(n_obs):
            for member in range(n_par):
                there = at ^ (half + k if member % 2 or not k else k)
                pairs.append((at * n_par + member, there * n_par + member))
        got.append(lax.ppermute(norm, ("obs", "par"), pairs))
    return exchanged(call(norm_kernel, jax.ShapeDtypeStruct(norm.shape, F32), (norm, *got)), "par", n_par, 1, 2)


def shards(n_obs, n_par, operator, targets, start):
    rows, columns = operator.shape
    scen = start.shape[0]
    near = 4 if n_obs % 4 == 0 else n_obs
    width = columns // near
    lanes = shape(scen, LANES)
    image_shape = shape(scen, rows)
    term_shape = shape(2 * scen, rows, dtype=BF16)

    def gradient_parts(w, norm, packed, before):
        order = slots(near, RS_ORDERS)
        got = [exchange_slot(backward(n_obs, near, d, op, w, packed), n_obs, n_par, d) for d in order]
        total = backward(n_obs, near, (0, 0), op, w)
        for piece in got[:-1]:
            total = call(add_kernel, shape(scen, width), (total, piece), flops=ADD_FLOPS)
        both = shape(scen, width + LANES, dtype=BF16)
        value = call(
            functools.partial(near_kernel, order, len(before)),
            both,
            (total, norm, *before, *got),
            [VMEM] * 2 + [ANY] * len(before) + [VMEM] * len(got),
        )
        parts = [value]
        for index, (stride, members) in enumerate(stages(n_obs, near)):
            if index:
                value = call(functools.partial(far_kernel, True), both, parts)
            if mirrored(n_obs, near):
                stride += 2
            parts = exchanged(value, "obs", n_obs, stride, members)
        return parts

    def image_parts(mine):
        got = [exchange_slot(mine, n_obs, n_par, d) for d in slots(near, AG_ORDERS)]
        total = forward(near == 1, turned[0], mine)
        for k, piece in enumerate(got):
            total = forward(k == len(got) - 1, turned[k + 1], piece, total)
        return parts_over(total, "par", n_par, True), [mine] + got

    op, first = load(operator, start)
    turned = [turn(n_obs, near, d, op) for d in [(0, 0)] + slots(near, AG_ORDERS)]
    packed_lanes = shape(scen, LANES, dtype=BF16)
    residual, w, norm, packed = call(
        first_kernel, (image_shape, term_shape, lanes, packed_lanes), (targets, *parts_over(first, "par", n_par, False))
    )
    images, alphas, betas, pieces = [], [], [], []
    gradient = gamma = None
    for index in range(ITERS):
        parts = gradient_parts(w, norm, packed, () if index else turned[:2])
        gradient, rounded, alpha = call(
            functools.partial(gradient_kernel, index > 0, near),
            (shape(scen, width), shape(scen, width, dtype=BF16), lanes),
            ((gradient, gamma) if index else tuple(turned)) + tuple(parts),
            None if index else [ANY] * near + [VMEM] * len(parts),
        )
        alphas += [alpha] if index else []
        parts, got = image_parts(rounded)
        pieces += got
        last = index == ITERS - 1
        image, gamma, beta, norm, *more = call(
            functools.partial(image_kernel, index > 0, last),
            (image_shape, lanes, lanes, lanes) + (() if last else (packed_lanes, term_shape)),
            ((image, gamma) if index else ()) + tuple(parts),
        )
        if not last:
            packed, w = more
        images.append(image)
        betas.append(beta)

    norms = norm_parts(norm, n_obs, n_par)
    direction, base = call(
        functools.partial(directions_kernel, n_obs, near, width),
        (shape(scen, columns), shape(scen, columns)),
        (start, *alphas, *betas, *pieces),
    )
    return call(
        functools.partial(last_kernel, len(norms)),
        (shape(scen, columns), image_shape),
        (gamma, direction, base, residual, *norms, *alphas, *images),
    )


def solution(mesh):
    return jax.shard_map(
        functools.partial(shards, mesh.shape["obs"], mesh.shape["par"]),
        mesh=mesh,
        in_specs=(P("obs", "par"), P(None, "obs"), P(None, "par")),
        out_specs=(P(None, "par"), P(None, "obs")),
        check_vma=False,
    )
```
